128 devices in a mesh: tile: 8 (over x, core), tm: 16 (over y, z).
Axes of the slice: x: 4, y: 4, z: 4, core: 2. Of those that a mesh axis runs over, the one named last changes fastest.
Arguments:
- movie: bfloat16 [256, 256, 1024], P('tile', None, 'tm'), may hold values from -6 to 6
- footprints: bfloat16 [64, 4, 32, 32, 128], P('tile'), may hold values from -0.5 to 0.5
- support: int32 [64, 4], P('tile'), may hold values from -1 to 31, as said below
- cycle_offsets: int32 [48, 2], replicated, may hold values from -8 to 8, as said below
- cycle_weights: float32 [48, 256, 256], P(None, 'tile'), may hold values from -0.875 to 0.875
- owner_map: int32 [32], replicated, may hold values from 0 to 31, each once
- traces_old: bfloat16 [4096, 1024], P(('tile', 'tm')), may hold values from 0 to 2
- taps: float32 [129], replicated, may hold values from -0.5 to 0.5
Outputs:
- residual: bfloat16 [256, 256, 1024], P('tile', None, 'tm')
- traces_new: bfloat16 [4096, 1024], P(('tile', 'tm'))
The draws below stay inside these ranges and needn't reach their ends.
Inputs may be any that keep to these rules, and one draw needn't show every extreme that they name: `support`: in every row the live slots come first and name distinct blocks; -1 marks the empty slots. Every tile has 1 to 4 live slots, and every tile row (the 8 tiles t with equal t // 8) has exactly 20 live slots in all. `cycle_offsets`: rows are distinct (row offset, column offset) pairs; each has max(|row offset|, |column offset|) between 6 and 8; one row offset is 8 and one is -8. `owner_map`: each block has its own position.
All inputs are finite; a program needn't handle non-finite values.
Results may differ from the reference program's by a relative error of at most 0.0075.
Values may be sent and summed in bfloat16 or wider, within the bound.
A program may use at most 128 MiB of HBM per device.

```python
import jax
import jax.numpy as jnp
from jax import lax

TILE = 32
TILES_DEV = 8
F_DEV = 64
BLOCK = 128
NBLK = 32
KSLOTS = 4
RAD = 8
CYCLE = 48
HALF = 64
ROWS = 256
COLS = 256
FRAMES = 1024
NEURONS = 4096
TILES = 64
NTAP = 129
LIVE_DEV = 20
N_TILE = 8
N_TM = 16


def draw_footprints(key, part):
    base_key, neuron_key, pixel_key = jax.random.split(jax.random.fold_in(key, 37), 3)
    draw_shape = (TILES, KSLOTS, TILE, TILE, BLOCK)
    base_values = jnp.clip(jax.random.normal(base_key, draw_shape, jnp.float32), -4.0, 4.0)
    neuron_scale = jnp.exp(jax.random.uniform(neuron_key, (TILES, KSLOTS, 1, 1, BLOCK), jnp.float32, jnp.log(0.3), jnp.log(3.0)))
    pixel_scale = jnp.exp(jax.random.uniform(pixel_key, (TILES, 1, TILE, TILE, 1), jnp.float32, jnp.log(0.5), jnp.log(2.0)))
    return jnp.clip(base_values * neuron_scale * pixel_scale / 32.0, -0.5, 0.5).astype(jnp.bfloat16)


def draw_support(key, part):
    count_key, block_key = jax.random.split(jax.random.fold_in(key, 11))
    groups_total = TILES // TILES_DEV
    extra_total = TILES_DEV * (KSLOTS - 1)
    count_keys = jax.random.split(count_key, groups_total)
    chosen_order = jax.vmap(lambda one_key: jax.random.permutation(one_key, extra_total))(count_keys)
    chosen = (chosen_order < LIVE_DEV - TILES_DEV).astype(jnp.int32)
    counts = 1 + jnp.sum(chosen.reshape(groups_total, TILES_DEV, KSLOTS - 1), axis=2).reshape(TILES)
    block_keys = jax.random.split(block_key, TILES)
    orders = jax.vmap(lambda one_key: jax.random.permutation(one_key, NBLK))(block_keys)[:, :KSLOTS]
    slot_number = jnp.arange(KSLOTS, dtype=jnp.int32)[None, :]
    return jnp.where(slot_number < counts[:, None], orders, -1).astype(jnp.int32)


def draw_cycle_offsets(key, part):
    score_key, top_key, bottom_key = jax.random.split(jax.random.fold_in(key, 23), 3)
    span_cells = 2 * RAD + 1
    cell_ids = jnp.arange(span_cells * span_cells, dtype=jnp.int32)
    delta_row = cell_ids // span_cells - RAD
    delta_col = cell_ids % span_cells - RAD
    radius = jnp.maximum(jnp.abs(delta_row), jnp.abs(delta_col))
    usable = (radius >= RAD - 2) & (jnp.abs(delta_row) < RAD)
    scores = jax.random.randint(score_key, (span_cells * span_cells,), 0, 1 << 20) * (span_cells * span_cells) + cell_ids
    scores = jnp.where(usable, scores, 1 << 30)
    picked = jnp.argsort(scores)[:CYCLE - 2]
    top_col = jax.random.randint(top_key, (1,), -RAD, RAD + 1)
    bottom_col = jax.random.randint(bottom_key, (1,), -RAD, RAD + 1)
    rows_part = jnp.concatenate([delta_row[picked], jnp.array([RAD, -RAD], jnp.int32)])
    cols_part = jnp.concatenate([delta_col[picked], top_col, bottom_col])
    return jnp.stack([rows_part, cols_part], axis=1).astype(jnp.int32)


def block_scale(rng, extent, cuts, low, high):
    factor_of = 1.0
    for axis_at, shards_of in cuts:
        heights = jax.random.uniform(jax.random.fold_in(jax.random.fold_in(rng, 6), axis_at), (shards_of,), jnp.float32, low / len(cuts), high / len(cuts))
        factor_of = factor_of * jnp.repeat(jnp.exp(heights), extent[axis_at] // shards_of).reshape((-1,) + (1,) * (len(extent) - 1 - axis_at))
    return factor_of


def gaussian(key, shape, deviation, bound, shards=(), kind=jnp.bfloat16):
    entries = jax.random.normal(key, shape, jnp.float32) * deviation
    if len(shards) > 0:
        entries = block_scale(key, shape, shards, -0.22, 0.18) * entries
    return jnp.clip(entries, min=-bound, max=bound).astype(kind)


def setup_inputs(seed: int = 0) -> dict:
    splits = jax.random.split(jax.random.key(seed), 9)
    movie = gaussian(splits[0], (ROWS, COLS, FRAMES), 1.0, 6.0, ((0, 8), (2, 16)))
    footprints = draw_footprints(jax.random.fold_in(splits[8], 71), 0)
    support = draw_support(jax.random.fold_in(splits[8], 71), 0)
    cycle_offsets = draw_cycle_offsets(jax.random.fold_in(splits[8], 71), 0)
    cycle_weights = gaussian(splits[4], (CYCLE, ROWS, COLS), CYCLE ** -0.5, 0.875, ((1, 8),), jnp.float32)
    owner_map = jax.random.permutation(splits[5], NBLK).astype(jnp.int32)
    traces_old = jnp.clip(2.0 * jax.random.uniform(splits[6], (NEURONS, FRAMES), jnp.float32) ** block_scale(splits[6], (NEURONS, FRAMES), ((0, 128),), -0.2, 0.2), 0.0, 2.0).astype(jnp.bfloat16)
    taps = gaussian(splits[7], (NTAP,), NTAP ** -0.5, 0.5, (), jnp.float32)
    return {"movie": movie, "footprints": footprints, "support": support, "cycle_offsets": cycle_offsets, "cycle_weights": cycle_weights, "owner_map": owner_map, "traces_old": traces_old, "taps": taps}


ridge_term = 1.0
highest = lax.Precision.HIGHEST


def cycle_pass(field_in, cycle_weights, cycle_offsets):
    row_count, col_count, frames = field_in.shape
    padded = jnp.pad(field_in.astype(jnp.float32), ((RAD, RAD), (RAD, RAD), (0, 0)))
    running = jnp.zeros((row_count, col_count, frames), jnp.float32)
    for cycle_index in range(CYCLE):
        start_row = (RAD + cycle_offsets[cycle_index, 0]).astype(jnp.int32)
        start_col = (RAD + cycle_offsets[cycle_index, 1]).astype(jnp.int32)
        shifted = lax.dynamic_slice(padded, (start_row, start_col, jnp.zeros((), jnp.int32)), (row_count, col_count, frames))
        running = running + cycle_weights[cycle_index][:, :, None] * shifted
    return running


def neural_part(footprint_f, live_slot, position, trace_block):
    frame_count = trace_block.shape[1]
    blocks = trace_block.reshape(NBLK, BLOCK, frame_count)
    picked = blocks[position.reshape(-1)].reshape(N_TILE, TILES_DEV, KSLOTS, BLOCK, frame_count)
    picked = jnp.where(live_slot.reshape(N_TILE, TILES_DEV, KSLOTS)[:, :, :, None, None], picked.astype(jnp.float32), 0.0)
    neural_image = jnp.einsum('gtkrcn,gtknf->grtcf', footprint_f, picked, precision=highest)
    return neural_image.reshape(ROWS, COLS, frame_count)


def reference(movie, footprints, support, cycle_offsets, cycle_weights, owner_map, traces_old, taps):
    live_slot = support >= 0
    position = owner_map[jnp.maximum(support, 0)].astype(jnp.int32)
    footprint_f = footprints.astype(jnp.float32).reshape(N_TILE, TILES_DEV, KSLOTS, TILE, TILE, BLOCK)
    block_ids = jnp.arange(NBLK, dtype=jnp.int32)
    selector = ((position.reshape(-1)[None, :] == block_ids[:, None]) & live_slot.reshape(-1)[None, :]).astype(jnp.float32)
    movie_blocks = movie.reshape(ROWS, COLS, N_TM, F_DEV).transpose(2, 0, 1, 3)
    old_blocks = traces_old.reshape(NEURONS, N_TM, F_DEV).transpose(1, 0, 2)

    def first_pass(carried):
        frame_movie, frame_traces = carried
        neural_old = neural_part(footprint_f, live_slot, position, frame_traces)
        first_res = (frame_movie.astype(jnp.float32) - neural_old).astype(jnp.bfloat16)
        second_res = (first_res.astype(jnp.float32) - cycle_pass(first_res, cycle_weights, cycle_offsets)).astype(jnp.bfloat16)
        third_res = (second_res.astype(jnp.float32) - cycle_pass(second_res, cycle_weights, cycle_offsets)).astype(jnp.bfloat16)
        tile_view = third_res.astype(jnp.float32).reshape(N_TILE, TILE, TILES_DEV, TILE, F_DEV)
        slot_proj = jnp.einsum('gtkrcn,grtcf->gtknf', footprint_f, tile_view, precision=highest)
        owned_sums = jnp.dot(selector, slot_proj.reshape(TILES * KSLOTS, BLOCK * F_DEV), precision=highest)
        return third_res, owned_sums.reshape(NEURONS, F_DEV)

    cleaned, projected = lax.map(first_pass, (movie_blocks, old_blocks))
    projected = projected.transpose(1, 0, 2).reshape(NEURONS, FRAMES)
    squares = jnp.sum(footprint_f * footprint_f, axis=(3, 4)).reshape(TILES * KSLOTS, BLOCK)
    norm_sums = jnp.dot(selector, squares, precision=highest).reshape(NEURONS)
    update = traces_old.astype(jnp.float32) + projected / (norm_sums[:, None] + ridge_term)
    padded = jnp.pad(update, ((0, 0), (HALF, HALF)))
    filtered = jnp.zeros((NEURONS, FRAMES), jnp.float32)
    for tap_index in range(2 * HALF + 1):
        begin_col = 2 * HALF - tap_index
        filtered = filtered + taps[tap_index] * padded[:, begin_col:begin_col + FRAMES]
    traces_new = jnp.maximum(filtered, 0.0).astype(jnp.bfloat16)
    new_blocks = traces_new.reshape(NEURONS, N_TM, F_DEV).transpose(1, 0, 2)

    def second_pass(carried):
        cleaned_block, frame_old, frame_new = carried
        image_old = neural_part(footprint_f, live_slot, position, frame_old)
        image_new = neural_part(footprint_f, live_slot, position, frame_new)
        return (cleaned_block.astype(jnp.float32) + image_old - image_new).astype(jnp.bfloat16)

    residual = lax.map(second_pass, (cleaned, old_blocks, new_blocks))
    residual = residual.transpose(1, 2, 0, 3).reshape(ROWS, COLS, FRAMES)
    return residual, traces_new
```

```python
import functools

import jax
import jax.numpy as jnp
from jax import lax
from jax.experimental import pallas as pl
from jax.experimental.pallas import tpu as pltpu
from jax.sharding import PartitionSpec as P

TILE = 32
BLOCK = 128
NBLK = 32
RAD = 8
RIDGE = 1.0
LANES = 128
FCHUNK = 32

SMEM = pltpu.MemorySpace.SMEM


def whole(space=pltpu.MemorySpace.VMEM):
    return pl.BlockSpec(memory_space=space)


def params(limit=48):
    return pltpu.CompilerParams(vmem_limit_bytes=limit * 2**20)


def block_of(support_ref, owner_ref, tile, slot):
    held = support_ref[tile, slot]
    return held >= 0, owner_ref[jnp.maximum(held, 0)]


def first_kernel(support_ref, owner_ref, traces_ref, foot_ref, movie_ref, out_ref, image):
    group = pl.program_id(0)
    tiles, slots = foot_ref.shape[0], foot_ref.shape[1]
    rows, width, frames = movie_ref.shape

    def one_tile(tile, carry):
        columns = pl.ds(pl.multiple_of(tile * TILE, TILE), TILE)
        for slot in range(slots):
            live, position = block_of(support_ref, owner_ref, group * tiles + tile, slot)

            def add(slot=slot, position=position):
                start = pl.multiple_of(position * BLOCK, BLOCK)
                part = jnp.dot(
                    foot_ref[tile, slot],
                    traces_ref[pl.ds(start, BLOCK), :],
                    preferred_element_type=jnp.float32,
                ).reshape(rows, TILE, frames)
                if slot == 0:
                    image[:, columns, :] = part
                else:
                    image[:, columns, :] += part

            if slot == 0:
                add()
            else:
                pl.when(live)(add)
        return carry

    lax.fori_loop(0, tiles, one_tile, 0)

    def two_rows(half, carry):
        row = half * 2
        both = [movie_ref[row + k].astype(jnp.float32) - image[row + k] for k in range(2)]
        turned = jnp.concatenate(both, axis=1).T
        for k in range(2):
            out_ref[row + k] = turned[k * frames : (k + 1) * frames].astype(jnp.bfloat16)
        return carry

    lax.fori_loop(0, rows // 2, two_rows, 0)


def first_residual(support, owner_map, traces, foot, movie):
    tiles, slots = foot.shape[:2]
    rows, cols, frames = movie.shape
    group = LANES // TILE
    return pl.pallas_call(
        first_kernel,
        grid=(tiles // group,),
        out_shape=jax.ShapeDtypeStruct((rows, frames, cols), jnp.bfloat16),
        in_specs=[
            whole(SMEM),
            whole(SMEM),
            whole(),
            pl.BlockSpec((group,) + foot.shape[1:], lambda g: (g, 0, 0, 0)),
            pl.BlockSpec((rows, LANES, frames), lambda g: (0, g, 0)),
        ],
        out_specs=pl.BlockSpec((rows, frames, LANES), lambda g: (0, 0, g)),
        scratch_shapes=[pltpu.VMEM((rows, LANES, frames), jnp.float32)],
        compiler_params=params(),
        name="first_residual",
    )(support, owner_map, traces, foot, movie)


def cycle_kernel(offsets_ref, weights_ref, field_ref, top_ref, bottom_ref, out_ref, padded):
    rows, frames, cols = field_ref.shape
    count = weights_ref.shape[1]
    padded[0:RAD] = top_ref[...].astype(jnp.float32)
    padded[RAD : RAD + rows] = field_ref[...].astype(jnp.float32)
    padded[RAD + rows : rows + 2 * RAD] = bottom_ref[...].astype(jnp.float32)
    lane = lax.broadcasted_iota(jnp.int32, (FCHUNK, LANES), 1)

    def one_row(row, carry):
        def one_chunk(chunk, inner):
            at = pl.ds(pl.multiple_of(chunk * FCHUNK, FCHUNK), FCHUNK)
            low = jnp.zeros((FCHUNK, LANES), jnp.float32)
            high = jnp.zeros((FCHUNK, LANES), jnp.float32)
            for j in range(count):
                down, right = offsets_ref[j, 0], offsets_ref[j, 1]
                source = RAD + row + down
                turn = lax.rem(LANES - right, LANES)
                first = pltpu.roll(padded[source, at, 0:LANES], turn, 1)
                second = pltpu.roll(padded[source, at, LANES : 2 * LANES], turn, 1)
                shifted = lane + right
                stays = (shifted >= 0) & (shifted < LANES)
                weight = weights_ref[row, j : j + 1, :]
                low += weight[:, :LANES] * jnp.where(stays, first, second)
                high += weight[:, LANES:] * jnp.where(stays, second, first)
            mine = padded[RAD + row, at, :]
            out_ref[row, at, 0:LANES] = (mine[:, :LANES] - low).astype(jnp.bfloat16)
            out_ref[row, at, LANES : 2 * LANES] = (mine[:, LANES:] - high).astype(jnp.bfloat16)
            return inner

        return lax.fori_loop(0, frames // FCHUNK, one_chunk, carry)

    lax.fori_loop(0, rows, one_row, 0)


def cycle_pass(offsets, weights, field, top, bottom):
    rows, frames, cols = field.shape
    return pl.pallas_call(
        cycle_kernel,
        out_shape=jax.ShapeDtypeStruct(field.shape, jnp.bfloat16),
        in_specs=[whole(SMEM)] + [whole()] * 4,
        out_specs=whole(),
        scratch_shapes=[pltpu.VMEM((rows + 2 * RAD, frames, cols), jnp.float32)],
        compiler_params=params(),
        name="cycle_pass",
    )(offsets, weights, field, top, bottom)


def project_kernel(support_ref, owner_ref, foot_ref, field_ref, third_ref, sums_ref, norms_ref):
    group = pl.program_id(0)
    tiles, slots, pixels, _ = foot_ref.shape
    rows, frames, width = field_ref.shape

    @pl.when(group == 0)
    def _():
        sums_ref[...] = jnp.zeros_like(sums_ref)
        norms_ref[...] = jnp.zeros_like(norms_ref)

    def two_rows(half, carry):
        row = half * 2
        both = field_ref[pl.ds(row, 2)].reshape(2 * frames, width).astype(jnp.float32)
        turned = both.T.astype(jnp.bfloat16)
        for k in range(2):
            third_ref[row + k] = turned[:, k * frames : (k + 1) * frames]
        return carry

    lax.fori_loop(0, rows // 2, two_rows, 0)

    def one_tile(tile, carry):
        columns = pl.ds(pl.multiple_of(tile * TILE, TILE), TILE)
        view = third_ref[:, columns, :].reshape(pixels, frames)
        for slot in range(slots):
            live, position = block_of(support_ref, owner_ref, group * tiles + tile, slot)

            def add(slot=slot, position=position):
                values = foot_ref[tile, slot]
                sums_ref[position] += lax.dot_general(
                    values, view, (((0,), (0,)), ((), ())), preferred_element_type=jnp.float32
                )
                wide = values.astype(jnp.float32)
                square = jnp.sum((wide * wide).reshape(pixels // 8, 8, BLOCK), axis=0)
                norms_ref[position] += square

            if slot == 0:
                add()
            else:
                pl.when(live)(add)
        return carry

    lax.fori_loop(0, tiles, one_tile, 0)


def project(support, owner_map, foot, field):
    tiles, slots = foot.shape[:2]
    rows, frames, cols = field.shape
    group = LANES // TILE
    return pl.pallas_call(
        project_kernel,
        grid=(tiles // group,),
        out_shape=[
            jax.ShapeDtypeStruct((rows, cols, frames), jnp.bfloat16),
            jax.ShapeDtypeStruct((NBLK, BLOCK, frames), jnp.float32),
            jax.ShapeDtypeStruct((NBLK, 8, BLOCK), jnp.float32),
        ],
        in_specs=[
            whole(SMEM),
            whole(SMEM),
            pl.BlockSpec((group,) + foot.shape[1:], lambda g: (g, 0, 0, 0)),
            pl.BlockSpec((rows, frames, LANES), lambda g: (0, 0, g)),
        ],
        out_specs=[
            pl.BlockSpec((rows, LANES, frames), lambda g: (0, g, 0)),
            pl.BlockSpec((NBLK, BLOCK, frames), lambda g: (0, 0, 0)),
            pl.BlockSpec((NBLK, 8, BLOCK), lambda g: (0, 0, 0)),
        ],
        compiler_params=params(),
        name="project",
    )(support, owner_map, foot, field)


def final_kernel(support_ref, owner_ref, old_ref, new_ref, foot_ref, third_ref, out_ref, change):
    tile = pl.program_id(0)
    slots = foot_ref.shape[1]
    rows, width, frames = third_ref.shape

    @pl.when(tile == 0)
    def _():
        change[...] = (
            old_ref[...].astype(jnp.float32) - new_ref[...].astype(jnp.float32)
        ).astype(jnp.bfloat16)

    def product(slot):
        live, position = block_of(support_ref, owner_ref, tile, slot)
        start = pl.multiple_of(position * BLOCK, BLOCK)
        part = change[pl.ds(start, BLOCK), :]
        part = jnp.where(live, part, jnp.zeros_like(part))
        return jnp.dot(foot_ref[0, slot], part, preferred_element_type=jnp.float32)

    total = product(0)
    for slot in range(1, slots):
        total += product(slot)
    out_ref[...] = (third_ref[...].astype(jnp.float32) + total.reshape(rows, width, frames)).astype(
        jnp.bfloat16
    )


def final_residual(support, owner_map, old, new, foot, third):
    tiles, slots = foot.shape[:2]
    rows, cols, frames = third.shape
    return pl.pallas_call(
        final_kernel,
        grid=(tiles,),
        out_shape=jax.ShapeDtypeStruct(third.shape, jnp.bfloat16),
        in_specs=[
            whole(SMEM),
            whole(SMEM),
            whole(),
            whole(),
            pl.BlockSpec((1,) + foot.shape[1:], lambda t: (t, 0, 0, 0)),
            pl.BlockSpec((rows, TILE, frames), lambda t: (0, t, 0)),
        ],
        out_specs=pl.BlockSpec((rows, TILE, frames), lambda t: (0, t, 0)),
        scratch_shapes=[pltpu.VMEM(old.shape, jnp.bfloat16)],
        compiler_params=params(),
        name="final_residual",
    )(support, owner_map, old, new, foot, third)


def filter_kernel(taps_ref, norms_ref, old_ref, sums_ref, out_ref, stacked):
    owned, frames = old_ref.shape
    update = old_ref[...].astype(jnp.float32) + sums_ref[...] / (norms_ref[...] + RIDGE)
    half = LANES // 2
    edge = jnp.zeros((owned, half), jnp.float32)
    padded = jnp.concatenate([edge, update, edge], axis=1)
    parts = frames // LANES
    for i in range(parts):
        stacked[i * owned : (i + 1) * owned] = padded[:, i * LANES : (i + 2) * LANES]
    table = pltpu.roll(
        jnp.broadcast_to(taps_ref[...], (LANES, 2 * LANES)), 0, 1, stride=1, stride_axis=0
    )
    made = lax.dot_general(
        stacked[...],
        table,
        (((1,), (1,)), ((), ())),
        precision=lax.Precision.HIGHEST,
        preferred_element_type=jnp.float32,
    )
    for i in range(parts):
        out_ref[:, i * LANES : (i + 1) * LANES] = jnp.maximum(
            made[i * owned : (i + 1) * owned], 0.0
        ).astype(jnp.bfloat16)


def filter_traces(taps, norms, old, sums):
    owned, frames = old.shape
    reversed_taps = jnp.pad(taps[::-1], (0, 2 * LANES - taps.shape[0]))[None, :]
    return pl.pallas_call(
        filter_kernel,
        out_shape=jax.ShapeDtypeStruct(old.shape, jnp.bfloat16),
        in_specs=[whole()] * 4,
        out_specs=whole(),
        scratch_shapes=[pltpu.VMEM((owned * frames // LANES, 2 * LANES), jnp.float32)],
        compiler_params=params(),
        name="filter_traces",
    )(reversed_taps, norms, old, sums)


def to_tiles(owned):
    group_traces = lax.all_to_all(owned, "tm", split_axis=1, concat_axis=0, tiled=True)
    return lax.all_gather(group_traces, "tile", axis=0, tiled=True)


def halos(field):
    peers = lax.axis_size("tile")
    up = [(i, i + 1) for i in range(peers - 1)]
    down = [(i + 1, i) for i in range(peers - 1)]
    return lax.ppermute(field[-RAD:], "tile", up), lax.ppermute(field[:RAD], "tile", down)


def body(movie, footprints, support, cycle_offsets, cycle_weights, owner_map, traces_old, taps):
    tiles, slots = support.shape
    time_count = lax.axis_size("tm")
    tile_count = lax.axis_size("tile")
    owned, frames_all = traces_old.shape
    frames = movie.shape[2]
    cols = movie.shape[1]
    foot = footprints.reshape(tiles, slots, TILE * TILE, BLOCK)
    place = jnp.arange(cols, dtype=jnp.int32)[None, :] + cycle_offsets[:, 1:2]
    inside = (place >= 0) & (place < cols)
    weights = jnp.where(inside[:, None, :], cycle_weights, 0.0).transpose(1, 0, 2)

    old_full = to_tiles(traces_old)
    first = first_residual(support, owner_map, old_full, foot, movie)
    second = cycle_pass(cycle_offsets, weights, first, *halos(first))
    third_turned = cycle_pass(cycle_offsets, weights, second, *halos(second))
    third, sums, squares = project(support, owner_map, foot, third_turned)
    norms = jnp.sum(squares, axis=1).reshape(NBLK * BLOCK)
    mine = lax.psum_scatter(
        sums.reshape(NBLK * BLOCK, frames), "tile", scatter_dimension=0, tiled=True
    )
    mine_norms = lax.psum_scatter(norms, "tile", scatter_dimension=0, tiled=True)
    owned_sums = lax.all_to_all(mine, "tm", split_axis=0, concat_axis=1, tiled=True)
    owned_norms = lax.dynamic_slice_in_dim(mine_norms, lax.axis_index("tm") * owned, owned)
    fresh = filter_traces(taps, owned_norms[:, None], traces_old, owned_sums)
    residual = final_residual(support, owner_map, old_full, to_tiles(fresh), foot, third)
    return (residual, fresh)


def solution(mesh):
    return jax.shard_map(
        body,
        mesh=mesh,
        in_specs=(
            P("tile", None, "tm"),
            P("tile", None, None, None, None),
            P("tile", None),
            P(),
            P(None, "tile", None),
            P(),
            P(("tile", "tm"), None),
            P(),
        ),
        out_specs=(P("tile", None, "tm"), P(("tile", "tm"), None)),
        check_vma=False,
    )
```

```python
import functools

import jax
import jax.numpy as jnp
from jax import lax
from jax.experimental import pallas as pl
from jax.experimental.pallas import tpu as pltpu
from jax.sharding import PartitionSpec as P

TILE = 32
BLOCK = 128
NBLK = 32
RAD = 8
RIDGE = 1.0
LANES = 128
FCHUNK = 32

SMEM = pltpu.MemorySpace.SMEM


def whole(space=pltpu.MemorySpace.VMEM):
    return pl.BlockSpec(memory_space=space)


def params(limit=48):
    return pltpu.CompilerParams(vmem_limit_bytes=limit * 2**20)


def block_of(support_ref, owner_ref, tile, slot):
    held = support_ref[tile, slot]
    return held >= 0, owner_ref[jnp.maximum(held, 0)]


def first_kernel(support_ref, owner_ref, traces_ref, foot_ref, movie_ref, out_ref, image):
    group = pl.program_id(0)
    tiles, slots = foot_ref.shape[0], foot_ref.shape[1]
    rows, width, frames = movie_ref.shape

    def one_tile(tile, carry):
        columns = pl.ds(pl.multiple_of(tile * TILE, TILE), TILE)
        for slot in range(slots):
            live, position = block_of(support_ref, owner_ref, group * tiles + tile, slot)

            def add(slot=slot, position=position):
                start = pl.multiple_of(position * (BLOCK // 2), BLOCK // 2)
                part = jnp.dot(
                    foot_ref[tile, slot],
                    unpack(traces_ref[pl.ds(start, BLOCK // 2), :]),
                    preferred_element_type=jnp.float32,
                ).reshape(rows, TILE, frames)
                if slot == 0:
                    image[:, columns, :] = part
                else:
                    image[:, columns, :] += part

            if slot == 0:
                add()
            else:
                pl.when(live)(add)
        return carry

    lax.fori_loop(0, tiles, one_tile, 0)

    def two_rows(half, carry):
        row = half * 2
        both = [movie_ref[row + k].astype(jnp.float32) - image[row + k] for k in range(2)]
        turned = jnp.concatenate(both, axis=1).T
        for k in range(2):
            out_ref[row + k] = turned[k * frames : (k + 1) * frames].astype(jnp.bfloat16)
        return carry

    lax.fori_loop(0, rows // 2, two_rows, 0)


def first_residual(support, owner_map, traces, foot, movie):
    tiles, slots = foot.shape[:2]
    rows, cols, frames = movie.shape
    group = LANES // TILE
    return pl.pallas_call(
        first_kernel,
        grid=(tiles // group,),
        out_shape=jax.ShapeDtypeStruct((rows, frames, cols), jnp.bfloat16),
        in_specs=[
            whole(SMEM),
            whole(SMEM),
            whole(),
            pl.BlockSpec((group,) + foot.shape[1:], lambda g: (g, 0, 0, 0)),
            pl.BlockSpec((rows, LANES, frames), lambda g: (0, g, 0)),
        ],
        out_specs=pl.BlockSpec((rows, frames, LANES), lambda g: (0, 0, g)),
        scratch_shapes=[pltpu.VMEM((rows, LANES, frames), jnp.float32)],
        compiler_params=params(),
        name="first_residual",
    )(support, owner_map, traces, foot, movie)


def cycle_kernel(offsets_ref, weights_ref, field_ref, top_ref, bottom_ref, out_ref, padded):
    rows, frames, cols = field_ref.shape
    count = weights_ref.shape[1]
    padded[0:RAD] = top_ref[...].astype(jnp.float32)
    padded[RAD : RAD + rows] = field_ref[...].astype(jnp.float32)
    padded[RAD + rows : rows + 2 * RAD] = bottom_ref[...].astype(jnp.float32)
    lane = lax.broadcasted_iota(jnp.int32, (FCHUNK, LANES), 1)

    def one_row(row, carry):
        def one_chunk(chunk, inner):
            at = pl.ds(pl.multiple_of(chunk * FCHUNK, FCHUNK), FCHUNK)
            low = jnp.zeros((FCHUNK, LANES), jnp.float32)
            high = jnp.zeros((FCHUNK, LANES), jnp.float32)
            for j in range(count):
                down, right = offsets_ref[j, 0], offsets_ref[j, 1]
                source = RAD + row + down
                turn = lax.rem(LANES - right, LANES)
                first = pltpu.roll(padded[source, at, 0:LANES], turn, 1)
                second = pltpu.roll(padded[source, at, LANES : 2 * LANES], turn, 1)
                shifted = lane + right
                stays = (shifted >= 0) & (shifted < LANES)
                weight = weights_ref[row, j : j + 1, :]
                low += weight[:, :LANES] * jnp.where(stays, first, second)
                high += weight[:, LANES:] * jnp.where(stays, second, first)
            mine = padded[RAD + row, at, :]
            out_ref[row, at, 0:LANES] = (mine[:, :LANES] - low).astype(jnp.bfloat16)
            out_ref[row, at, LANES : 2 * LANES] = (mine[:, LANES:] - high).astype(jnp.bfloat16)
            return inner

        return lax.fori_loop(0, frames // FCHUNK, one_chunk, carry)

    lax.fori_loop(0, rows, one_row, 0)


def cycle_pass(offsets, weights, field, top, bottom):
    rows, frames, cols = field.shape
    return pl.pallas_call(
        cycle_kernel,
        out_shape=jax.ShapeDtypeStruct(field.shape, jnp.bfloat16),
        in_specs=[whole(SMEM)] + [whole()] * 4,
        out_specs=whole(),
        scratch_shapes=[pltpu.VMEM((rows + 2 * RAD, frames, cols), jnp.float32)],
        compiler_params=params(),
        name="cycle_pass",
    )(offsets, weights, field, top, bottom)


def project_kernel(
    support_ref, owner_ref, foot_ref, field_ref, third_ref, packed_ref, sums_ref, norms_ref
):
    group = pl.program_id(0)
    tiles, slots, pixels, _ = foot_ref.shape
    rows, frames, width = field_ref.shape

    @pl.when(group == 0)
    def _():
        sums_ref[...] = jnp.zeros_like(sums_ref)
        norms_ref[...] = jnp.zeros_like(norms_ref)

    def two_rows(half, carry):
        row = half * 2
        both = field_ref[pl.ds(row, 2)].reshape(2 * frames, width).astype(jnp.float32)
        turned = both.T.astype(jnp.bfloat16)
        for k in range(2):
            third_ref[row + k] = turned[:, k * frames : (k + 1) * frames]
        return carry

    lax.fori_loop(0, rows // 2, two_rows, 0)

    def one_tile(tile, carry):
        columns = pl.ds(pl.multiple_of(tile * TILE, TILE), TILE)
        view = third_ref[:, columns, :].reshape(pixels, frames)
        for slot in range(slots):
            live, position = block_of(support_ref, owner_ref, group * tiles + tile, slot)

            def add(slot=slot, position=position):
                values = foot_ref[tile, slot]
                sums_ref[position] += lax.dot_general(
                    values, view, (((0,), (0,)), ((), ())), preferred_element_type=jnp.float32
                )
                wide = values.astype(jnp.float32)
                square = jnp.sum((wide * wide).reshape(pixels // 8, 8, BLOCK), axis=0)
                norms_ref[position] += square

            if slot == 0:
                add()
            else:
                pl.when(live)(add)
        return carry

    lax.fori_loop(0, tiles, one_tile, 0)

    @pl.when(group == pl.num_programs(0) - 1)
    def _():
        each = packed_ref.shape[2] - PACK
        per = each // (BLOCK // 2)
        for core in range(packed_ref.shape[0]):

            def one_chip(chip, carry, core=core):
                base = (2 * chip + core) * per
                for q in range(per):
                    values = sums_ref[base + q]
                    for k in range(BLOCK // (2 * PACK)):
                        top = values[2 * k * PACK : (2 * k + 1) * PACK]
                        bottom = values[(2 * k + 1) * PACK : (2 * k + 2) * PACK]
                        packed_ref[
                            core, chip, q * (BLOCK // 2) + k * PACK : q * (BLOCK // 2) + (k + 1) * PACK
                        ] = jnp.concatenate([top, bottom], axis=1).astype(jnp.bfloat16)
                lines = [jnp.sum(norms_ref[base + q], axis=0, keepdims=True) for q in range(per)]
                fill = [jnp.zeros((PACK // 2 - per, BLOCK), jnp.float32)]
                norms = jnp.concatenate(lines + fill, axis=0)
                high = norms.astype(jnp.bfloat16).astype(jnp.float32)
                packed_ref[core, chip, each : each + PACK] = jnp.concatenate(
                    [high, norms - high], axis=0
                ).astype(jnp.bfloat16)
                return carry

            lax.fori_loop(0, packed_ref.shape[1], one_chip, 0)


def project(support, owner_map, foot, field):
    tiles, slots = foot.shape[:2]
    rows, frames, cols = field.shape
    group = LANES // TILE
    packed = (2, lax.axis_size("tile") // 2, lax.axis_size("tm") * PACK + PACK, LANES)
    return pl.pallas_call(
        project_kernel,
        grid=(tiles // group,),
        out_shape=[
            jax.ShapeDtypeStruct((rows, cols, frames), jnp.bfloat16),
            jax.ShapeDtypeStruct(packed, jnp.bfloat16),
        ],
        in_specs=[
            whole(SMEM),
            whole(SMEM),
            pl.BlockSpec((group,) + foot.shape[1:], lambda g: (g, 0, 0, 0)),
            pl.BlockSpec((rows, frames, LANES), lambda g: (0, 0, g)),
        ],
        out_specs=[
            pl.BlockSpec((rows, LANES, frames), lambda g: (0, g, 0)),
            pl.BlockSpec(packed, lambda g: (0, 0, 0, 0)),
        ],
        scratch_shapes=[
            pltpu.VMEM((NBLK, BLOCK, frames), jnp.float32),
            pltpu.VMEM((NBLK, 8, BLOCK), jnp.float32),
        ],
        compiler_params=params(),
        name="project",
    )(support, owner_map, foot, field)


def final_kernel(support_ref, owner_ref, old_ref, new_ref, foot_ref, third_ref, out_ref, change):
    tile = pl.program_id(0)
    slots = foot_ref.shape[1]
    rows, width, frames = third_ref.shape

    @pl.when(tile == 0)
    def _():
        change[...] = (
            old_ref[...].astype(jnp.float32) - new_ref[...].astype(jnp.float32)
        ).astype(jnp.bfloat16)

    def product(slot):
        live, position = block_of(support_ref, owner_ref, tile, slot)
        start = pl.multiple_of(position * (BLOCK // 2), BLOCK // 2)
        part = unpack(change[pl.ds(start, BLOCK // 2), :])
        part = jnp.where(live, part, jnp.zeros_like(part))
        return jnp.dot(foot_ref[0, slot], part, preferred_element_type=jnp.float32)

    total = product(0)
    for slot in range(1, slots):
        total += product(slot)
    out_ref[...] = (third_ref[...].astype(jnp.float32) + total.reshape(rows, width, frames)).astype(
        jnp.bfloat16
    )


def final_residual(support, owner_map, old, new, foot, third):
    tiles, slots = foot.shape[:2]
    rows, cols, frames = third.shape
    return pl.pallas_call(
        final_kernel,
        grid=(tiles,),
        out_shape=jax.ShapeDtypeStruct(third.shape, jnp.bfloat16),
        in_specs=[
            whole(SMEM),
            whole(SMEM),
            whole(),
            whole(),
            pl.BlockSpec((1,) + foot.shape[1:], lambda t: (t, 0, 0, 0)),
            pl.BlockSpec((rows, TILE, frames), lambda t: (0, t, 0)),
        ],
        out_specs=pl.BlockSpec((rows, TILE, frames), lambda t: (0, t, 0)),
        scratch_shapes=[pltpu.VMEM(old.shape, jnp.bfloat16)],
        compiler_params=params(),
        name="final_residual",
    )(support, owner_map, old, new, foot, third)


MESH = pl.DeviceIdType.MESH
PACK = 16
HALF_LANES = LANES // 2


def low_lanes():
    return lax.broadcasted_iota(jnp.int32, (PACK, LANES), 1) < HALF_LANES


def join_low(left, right):
    return jnp.where(low_lanes(), left, pltpu.roll(right, HALF_LANES, 1))


def join_high(left, right):
    return jnp.where(low_lanes(), pltpu.roll(left, HALF_LANES, 1), right)


def chunks_of(top, bottom):
    return join_low(top, bottom), join_high(top, bottom)


def unpack(packed):
    wide = packed.astype(jnp.float32)
    turned = pltpu.roll(wide, HALF_LANES, 1)
    parts = []
    for k in range(packed.shape[0] // PACK):
        rows = slice(k * PACK, (k + 1) * PACK)
        parts += [wide[rows, :HALF_LANES], turned[rows, :HALF_LANES]]
    return jnp.concatenate(parts, axis=0).astype(jnp.bfloat16)


class Place:
    def __init__(self, tiles, times):
        self.chips, self.times = tiles // 2, times
        self.tile, self.time = lax.axis_index("tile"), lax.axis_index("tm")
        self.chip, self.core = self.tile // 2, lax.rem(self.tile, 2)
        self.sibling = self.chip * 2 + 1 - self.core

    def chip_at(self, step):
        return lax.rem(self.chip + step + self.chips, self.chips)

    def time_at(self, step):
        return lax.rem(self.time + step + self.times, self.times)

    def greet(self):
        barrier = pltpu.get_barrier_semaphore()
        peers = [(self.sibling, self.time)]
        peers += [(self.chip_at(d) * 2 + self.core, self.time) for d in range(1, self.chips)]
        peers += [(self.tile, self.time_at(d)) for d in range(1, self.times)]
        for peer in peers:
            pl.semaphore_signal(barrier, inc=1, device_id=peer, device_id_type=MESH)
        pl.semaphore_wait(barrier, len(peers))


def send(source, target, send_sem, recv_sem, device):
    return pltpu.make_async_remote_copy(
        src_ref=source,
        dst_ref=target,
        send_sem=send_sem,
        recv_sem=recv_sem,
        device_id=device,
        device_id_type=MESH,
    )


def spread(place, chunks, full, sems):
    (ts, tr), (xs, xr), (ss, sr) = sems
    tile, time = place.tile, place.time

    def rows(index):
        return pl.ds(pl.multiple_of(index * PACK, PACK), PACK)

    first = []
    for d in range(1, place.times):
        peer = place.time_at(d)
        copy = send(
            chunks.at[peer], full.at[tile, rows(time)], ts.at[d], tr.at[d], (tile, peer)
        )
        copy.start()
        first.append(copy)
    full[tile, rows(time)] = chunks[time]
    for d, copy in enumerate(first, 1):
        came = place.time_at(-d)
        send(
            chunks.at[time], full.at[tile, rows(came)], ts.at[d], tr.at[d], (tile, came)
        ).wait_recv()
    second = []
    for d in range(1, place.chips):
        copy = send(
            full.at[tile],
            full.at[tile],
            xs.at[d],
            xr.at[d],
            (place.chip_at(d) * 2 + place.core, time),
        )
        copy.start()
        second.append(copy)
    third = []
    for d in range(place.chips):
        came = place.chip_at(-d) * 2 + place.core
        if d:
            send(full.at[came], full.at[came], xs.at[d], xr.at[d], (came, time)).wait_recv()
        copy = send(
            full.at[came], full.at[came], ss.at[d], sr.at[d], (place.sibling, time)
        )
        copy.start()
        third.append(copy)
    for d in range(place.chips):
        came = place.chip_at(-d) * 2 + 1 - place.core
        send(
            full.at[came], full.at[came], ss.at[d], sr.at[d], (place.sibling, time)
        ).wait_recv()
    for copy in first + second + third:
        copy.wait_send()


def pair_sems(*counts):
    return [pltpu.SemaphoreType.DMA((n,)) for n in counts for _ in range(2)]


def pairs(sems):
    return [(sems[2 * k], sems[2 * k + 1]) for k in range(len(sems) // 2)]


def old_kernel(tiles, times, old_ref, full_ref, chunks, *sems):
    place = Place(tiles, times)
    for i in range(times // 2):
        part = old_ref[:, i * LANES : (i + 1) * LANES].astype(jnp.float32)
        even, odd = chunks_of(part[:PACK], part[PACK:])
        chunks[2 * i] = even.astype(jnp.bfloat16)
        chunks[2 * i + 1] = odd.astype(jnp.bfloat16)
    place.greet()
    spread(place, chunks, full_ref, pairs(sems))


def remote_params(identity):
    return pltpu.CompilerParams(
        vmem_limit_bytes=48 * 2**20, collective_id=identity, has_side_effects=True
    )


def spread_old(traces_old):
    tiles, times = lax.axis_size("tile"), lax.axis_size("tm")
    return pl.pallas_call(
        functools.partial(old_kernel, tiles, times),
        out_shape=jax.ShapeDtypeStruct((tiles, times * PACK, LANES), jnp.bfloat16),
        in_specs=[whole()],
        out_specs=whole(),
        scratch_shapes=[pltpu.VMEM((times, PACK, LANES), jnp.bfloat16)]
        + pair_sems(times, tiles // 2, tiles // 2),
        compiler_params=remote_params(0),
        name="spread_old",
    )(traces_old)


def exchange_kernel(
    tiles, times, taps_ref, old_ref, sums_ref, full_ref, fresh_ref,
    pair_buf, x_send, x_buf, owner_send, owner_buf, stacked, chunks, *sems
):
    place = Place(tiles, times)
    (ps, pr), (xs, xr), (ts, tr), *rest = pairs(sems)
    chips, tile, time, core = place.chips, place.tile, place.time, place.core
    rows = times * PACK
    place.greet()
    to_pair = []
    for d in [*range(1, chips), 0]:
        at = place.chip_at(d)
        copy = send(
            sums_ref.at[1 - core, at], pair_buf.at[at], ps.at[d], pr.at[d], (place.sibling, time)
        )
        copy.start()
        to_pair.append((d, at, copy))
    to_chip = []
    mine = None
    for d, at, copy in to_pair:
        copy.wait_recv()
        total = sums_ref[core, at].astype(jnp.float32) + pair_buf[at].astype(jnp.float32)
        if d:
            x_send[d] = total.astype(jnp.bfloat16)
            out = send(x_send.at[d], x_buf.at[d], xs.at[d], xr.at[d], (at * 2 + core, time))
            out.start()
            to_chip.append(out)
        else:
            mine = total
    for d, copy in enumerate(to_chip, 1):
        copy.wait_recv()
        mine += x_buf[d].astype(jnp.float32)
    owner_send[...] = mine[:rows].reshape(times, PACK, LANES)
    to_owner = []
    for d in range(1, times):
        peer = place.time_at(d)
        copy = send(owner_send.at[peer], owner_buf.at[time], ts.at[d], tr.at[d], (tile, peer))
        copy.start()
        to_owner.append(copy)
    owner_buf[time] = owner_send[time]

    high = mine[rows : rows + PACK]
    both = high + pltpu.roll(high, PACK - PACK // 2, 0)
    block = lax.rem(time * 2 * PACK, BLOCK)
    line = lax.broadcasted_iota(jnp.int32, (PACK, LANES), 0)
    lane = lax.broadcasted_iota(jnp.int32, (PACK, LANES), 1)
    row = jnp.sum(
        jnp.where(line == time // (BLOCK // (2 * PACK)), both, 0.0), axis=0, keepdims=True
    )
    columns = [
        jnp.sum(jnp.where(lane == line + block + k * PACK, row, 0.0), axis=1, keepdims=True)
        for k in range(2)
    ]
    divisor = jnp.where(lane < HALF_LANES, columns[0], columns[1]) + RIDGE

    for d in range(1, times):
        came = place.time_at(-d)
        send(
            owner_send.at[came], owner_buf.at[came], ts.at[d], tr.at[d], (tile, came)
        ).wait_recv()
    update = [jnp.zeros((PACK, LANES), jnp.float32)]
    for i in range(times // 2):
        part = old_ref[:, i * LANES : (i + 1) * LANES].astype(jnp.float32)
        for k, old in enumerate(chunks_of(part[:PACK], part[PACK:])):
            update.append(old + owner_buf[2 * i + k] / divisor)
    update.append(jnp.zeros((PACK, LANES), jnp.float32))
    steps = times // 2
    lines = [
        (join_low(update[2 * i], update[2 * i + 1]), join_high(update[2 * i], update[2 * i + 1]))
        for i in range(steps + 1)
    ]
    for i in range(steps):
        for k in range(2):
            at = slice((2 * i + k) * PACK, (2 * i + k + 1) * PACK)
            stacked[at, :LANES] = lines[i][k]
            stacked[at, LANES:] = lines[i + 1][k]
    table = pltpu.roll(
        jnp.broadcast_to(taps_ref[...], (LANES, 2 * LANES)), 0, 1, stride=1, stride_axis=0
    )
    made = lax.dot_general(
        stacked[...],
        table,
        (((1,), (1,)), ((), ())),
        precision=lax.Precision.HIGHEST,
        preferred_element_type=jnp.float32,
    )
    made = jnp.maximum(made, 0.0)
    for i in range(steps):
        part = made[2 * i * PACK : (2 * i + 2) * PACK]
        fresh_ref[:, i * LANES : (i + 1) * LANES] = part.astype(jnp.bfloat16)
        even, odd = chunks_of(part[:PACK], part[PACK:])
        chunks[2 * i] = even.astype(jnp.bfloat16)
        chunks[2 * i + 1] = odd.astype(jnp.bfloat16)
    spread(place, chunks, full_ref, rest)
    for copy in [c for _, _, c in to_pair] + to_chip + to_owner:
        copy.wait_send()


def exchange(taps, traces_old, sums):
    tiles, times = lax.axis_size("tile"), lax.axis_size("tm")
    chips = tiles // 2
    rows = times * PACK
    group = (rows + PACK, LANES)
    reversed_taps = jnp.pad(taps[::-1], (0, 2 * LANES - taps.shape[0]))[None, :]
    return pl.pallas_call(
        functools.partial(exchange_kernel, tiles, times),
        out_shape=[
            jax.ShapeDtypeStruct((tiles, rows, LANES), jnp.bfloat16),
            jax.ShapeDtypeStruct(traces_old.shape, jnp.bfloat16),
        ],
        in_specs=[whole()] * 3,
        out_specs=[whole()] * 2,
        scratch_shapes=[
            pltpu.VMEM((chips,) + group, jnp.bfloat16),
            pltpu.VMEM((chips,) + group, jnp.bfloat16),
            pltpu.VMEM((chips,) + group, jnp.bfloat16),
            pltpu.VMEM((times, PACK, LANES), jnp.float32),
            pltpu.VMEM((times, PACK, LANES), jnp.float32),
            pltpu.VMEM((times * PACK, 2 * LANES), jnp.float32),
            pltpu.VMEM((times, PACK, LANES), jnp.bfloat16),
        ]
        + pair_sems(chips, chips, times, times, chips, chips),
        compiler_params=remote_params(1),
        name="exchange",
    )(reversed_taps, traces_old, sums)


def halos(field):
    peers = lax.axis_size("tile")
    up = [(i, i + 1) for i in range(peers - 1)]
    down = [(i + 1, i) for i in range(peers - 1)]
    return lax.ppermute(field[-RAD:], "tile", up), lax.ppermute(field[:RAD], "tile", down)


def body(movie, footprints, support, cycle_offsets, cycle_weights, owner_map, traces_old, taps):
    tiles, slots = support.shape
    cols = movie.shape[1]
    foot = footprints.reshape(tiles, slots, TILE * TILE, BLOCK)
    place = jnp.arange(cols, dtype=jnp.int32)[None, :] + cycle_offsets[:, 1:2]
    inside = (place >= 0) & (place < cols)
    weights = jnp.where(inside[:, None, :], cycle_weights, 0.0).transpose(1, 0, 2)

    old_full = spread_old(traces_old).reshape(-1, LANES)
    first = first_residual(support, owner_map, old_full, foot, movie)
    second = cycle_pass(cycle_offsets, weights, first, *halos(first))
    third_turned = cycle_pass(cycle_offsets, weights, second, *halos(second))
    third, sums = project(support, owner_map, foot, third_turned)
    new_full, fresh = exchange(taps, traces_old, sums)
    residual = final_residual(
        support, owner_map, old_full, new_full.reshape(-1, LANES), foot, third
    )
    return (residual, fresh)


def solution(mesh):
    return jax.shard_map(
        body,
        mesh=mesh,
        in_specs=(
            P("tile", None, "tm"),
            P("tile", None, None, None, None),
            P("tile", None),
            P(),
            P(None, "tile", None),
            P(),
            P(("tile", "tm"), None),
            P(),
        ),
        out_specs=(P("tile", None, "tm"), P(("tile", "tm"), None)),
        check_vma=False,
    )
```

```python
import functools

import jax
import jax.numpy as jnp
from jax import lax
from jax.experimental import pallas as pl
from jax.experimental.pallas import tpu as pltpu
from jax.sharding import PartitionSpec as P

TILE = 32
BLOCK = 128
NBLK = 32
RAD = 8
RIDGE = 1.0
GROUP = 4
LANES = 128

SMEM = pltpu.MemorySpace.SMEM


def whole(space=pltpu.MemorySpace.VMEM):
    return pl.BlockSpec(memory_space=space)


def params(limit):
    return pltpu.CompilerParams(vmem_limit_bytes=limit * 2**20)


def block_of(support_ref, owner_ref, tile, slot):
    held = support_ref[slot, tile]
    return held >= 0, owner_ref[jnp.maximum(held, 0)]


def image_kernel(sign, both, support_ref, owner_ref, *refs):
    traces_refs, (foot_ref, field_ref, out_ref, image) = refs[: 1 + both], refs[1 + both :]
    tiles, slots = foot_ref.shape[0], foot_ref.shape[1]
    rows, frames, cols = field_ref.shape
    group = LANES // TILE

    def block(tile, slot):
        live, position = block_of(support_ref, owner_ref, tile, slot)
        at = pl.ds(pl.multiple_of(position * (BLOCK // 2), BLOCK // 2), BLOCK // 2)
        if both:
            old, new = [ref[at, :].astype(jnp.float32) for ref in traces_refs]
            part = unpack(old - new)
        else:
            part = unpack(traces_refs[0][at, :])
        return jnp.where(live, part, jnp.zeros_like(part))

    def pair(tile, slot):
        return jnp.dot(
            jnp.concatenate([foot_ref[tile, slot], foot_ref[tile, slot + 1]], axis=1),
            jnp.concatenate([block(tile, slot), block(tile, slot + 1)], axis=0),
            preferred_element_type=jnp.float32,
        ).reshape(rows, TILE, frames)

    for strip in range(cols // LANES):
        lanes = slice(strip * LANES, (strip + 1) * LANES)

        def one_tile(inner, carry, strip=strip):
            tile = strip * group + inner
            columns = pl.ds(pl.multiple_of(inner * TILE, TILE), TILE)
            image[:, columns, :] = pair(tile, 0)
            for slot in range(2, slots, 2):

                @pl.when(support_ref[slot, tile] >= 0)
                def _(slot=slot):
                    image[:, columns, :] += pair(tile, slot)

            return carry

        lax.fori_loop(0, group, one_tile, 0)

        def some_rows(step, carry, lanes=lanes):
            for u in range(0, 2 * GROUP, 2):
                row = step * 2 * GROUP + u
                turned = jnp.concatenate([image[row], image[row + 1]], axis=1).T
                for k in range(2):
                    part = turned[k * frames : (k + 1) * frames]
                    out_ref[row + k, :, lanes] = (
                        field_ref[row + k, :, lanes].astype(jnp.float32) + sign * part
                    ).astype(jnp.bfloat16)
            return carry

        lax.fori_loop(0, rows // (2 * GROUP), some_rows, 0)


def add_image(sign, support, owner_map, traces, foot, field, name):
    rows, frames, cols = field.shape
    return pl.pallas_call(
        functools.partial(image_kernel, sign, len(traces) - 1),
        out_shape=jax.ShapeDtypeStruct(field.shape, jnp.bfloat16),
        in_specs=[whole(SMEM), whole(SMEM)] + [whole() for _ in range(len(traces) + 2)],
        out_specs=whole(),
        scratch_shapes=[pltpu.VMEM((rows, LANES, frames), jnp.float32)],
        compiler_params=params(20),
        name=name,
    )(support, owner_map, *traces, foot, field)


def project_kernel(
    support_ref, owner_ref, foot_ref, field_ref, packed_ref, view, sums_ref, norms_ref
):
    tiles, slots, pixels, _ = foot_ref.shape
    rows, frames, cols = field_ref.shape
    group = LANES // TILE
    sums_ref[...] = jnp.zeros_like(sums_ref)
    norms_ref[...] = jnp.zeros_like(norms_ref)
    lane = lax.broadcasted_iota(jnp.int32, (frames, LANES), 1)

    def add(tile, slot):
        both = jnp.dot(
            view[lax.rem(tile, group)],
            jnp.concatenate([foot_ref[tile, slot], foot_ref[tile, slot + 1]], axis=1),
            preferred_element_type=jnp.float32,
        )
        for k in range(2):
            live, position = block_of(support_ref, owner_ref, tile, slot + k)
            part = both[:, k * BLOCK : (k + 1) * BLOCK]
            sums_ref[position] += jnp.where(live, part, 0.0)
            wide = foot_ref[tile, slot + k].astype(jnp.float32)
            square = jnp.sum((wide * wide).reshape(pixels // 8, 8, BLOCK), axis=0)
            norms_ref[position] += jnp.where(live, square, 0.0)

    for strip in range(cols // LANES):
        lanes = slice(strip * LANES, (strip + 1) * LANES)

        def some_rows(step, carry, lanes=lanes):
            source = [
                field_ref[step * group + k, :, lanes].astype(jnp.float32) for k in range(group)
            ]
            at = pl.ds(pl.multiple_of(step * LANES, LANES), LANES)
            for t in range(group):
                line = None
                for k in range(group):
                    shift = (k - t) * TILE % LANES
                    moved = pltpu.roll(source[k], shift, 1) if shift else source[k]
                    line = moved if k == 0 else jnp.where(lane >= k * TILE, moved, line)
                view[t, :, at] = line.astype(jnp.bfloat16)
            return carry

        lax.fori_loop(0, rows // group, some_rows, 0)

        def one_tile(inner, carry, strip=strip):
            tile = strip * group + inner
            add(tile, 0)
            for slot in range(2, slots, 2):

                @pl.when(support_ref[slot, tile] >= 0)
                def _(slot=slot):
                    add(tile, slot)

            return carry

        lax.fori_loop(0, group, one_tile, 0)

    each = packed_ref.shape[2] - PACK
    per = each // (BLOCK // 2)
    for core in range(packed_ref.shape[0]):

        def one_chip(chip, carry, core=core):
            base = (2 * chip + core) * per
            for q in range(per):
                values = sums_ref[base + q].T
                for k in range(BLOCK // (2 * PACK)):
                    top = values[2 * k * PACK : (2 * k + 1) * PACK]
                    bottom = values[(2 * k + 1) * PACK : (2 * k + 2) * PACK]
                    at = q * (BLOCK // 2) + k * PACK
                    packed_ref[core, chip, at : at + PACK] = jnp.concatenate(
                        [top, bottom], axis=1
                    ).astype(jnp.bfloat16)
            lines = [jnp.sum(norms_ref[base + q], axis=0, keepdims=True) for q in range(per)]
            fill = [jnp.zeros((PACK // 2 - per, BLOCK), jnp.float32)]
            norms = jnp.concatenate(lines + fill, axis=0)
            high = norms.astype(jnp.bfloat16).astype(jnp.float32)
            packed_ref[core, chip, each : each + PACK] = jnp.concatenate(
                [high, norms - high], axis=0
            ).astype(jnp.bfloat16)
            return carry

        lax.fori_loop(0, packed_ref.shape[1], one_chip, 0)


def project(support, owner_map, foot, field, chips, times):
    rows, frames, cols = field.shape
    return pl.pallas_call(
        project_kernel,
        out_shape=jax.ShapeDtypeStruct((2, chips, times * PACK + PACK, LANES), jnp.bfloat16),
        in_specs=[whole(SMEM), whole(SMEM), whole(), whole()],
        out_specs=whole(),
        scratch_shapes=[
            pltpu.VMEM((LANES // TILE, frames, TILE * TILE), jnp.bfloat16),
            pltpu.VMEM((NBLK, frames, BLOCK), jnp.float32),
            pltpu.VMEM((NBLK, 8, BLOCK), jnp.float32),
        ],
        compiler_params=params(20),
        name="project",
    )(support, owner_map, foot, field)


MESH = pl.DeviceIdType.MESH
PACK = 16
HALF_LANES = LANES // 2


def low_lanes():
    return lax.broadcasted_iota(jnp.int32, (PACK, LANES), 1) < HALF_LANES


def join_low(left, right):
    return jnp.where(low_lanes(), left, pltpu.roll(right, HALF_LANES, 1))


def join_high(left, right):
    return jnp.where(low_lanes(), pltpu.roll(left, HALF_LANES, 1), right)


def chunks_of(top, bottom):
    return join_low(top, bottom), join_high(top, bottom)


def unpack(packed):
    wide = packed.astype(jnp.float32)
    turned = pltpu.roll(wide, HALF_LANES, 1)
    parts = []
    for k in range(packed.shape[0] // PACK):
        rows = slice(k * PACK, (k + 1) * PACK)
        parts += [wide[rows, :HALF_LANES], turned[rows, :HALF_LANES]]
    return jnp.concatenate(parts, axis=0).astype(jnp.bfloat16)


class Place:
    def __init__(self, tiles, times):
        self.chips, self.times = tiles // 2, times
        self.tile, self.time = lax.axis_index("tile"), lax.axis_index("tm")
        self.chip, self.core = self.tile // 2, lax.rem(self.tile, 2)
        self.sibling = self.chip * 2 + 1 - self.core

    def chip_at(self, step):
        return lax.rem(self.chip + step + self.chips, self.chips)

    def time_at(self, step):
        return lax.rem(self.time + step + self.times, self.times)

    def greet(self):
        barrier = pltpu.get_barrier_semaphore()
        peers = [(self.sibling, self.time)]
        peers += [(self.chip_at(d) * 2 + self.core, self.time) for d in range(1, self.chips)]
        peers += [(self.tile, self.time_at(d)) for d in range(1, self.times)]
        for peer in peers:
            pl.semaphore_signal(barrier, inc=1, device_id=peer, device_id_type=MESH)
        pl.semaphore_wait(barrier, len(peers))


def send(source, target, send_sem, recv_sem, device):
    return pltpu.make_async_remote_copy(
        src_ref=source,
        dst_ref=target,
        send_sem=send_sem,
        recv_sem=recv_sem,
        device_id=device,
        device_id_type=MESH,
    )


def spread(place, chunks, full, sems, meanwhile=None):
    (ts, tr), (xs, xr), (ss, sr) = sems
    tile, time = place.tile, place.time

    def rows(index):
        return pl.ds(pl.multiple_of(index * PACK, PACK), PACK)

    first = []
    for d in range(1, place.times):
        peer = place.time_at(d)
        copy = send(
            chunks.at[peer], full.at[tile, rows(time)], ts.at[d], tr.at[d], (tile, peer)
        )
        copy.start()
        first.append(copy)
    full[tile, rows(time)] = chunks[time]
    if meanwhile:
        meanwhile()
    for d, copy in enumerate(first, 1):
        came = place.time_at(-d)
        send(
            chunks.at[time], full.at[tile, rows(came)], ts.at[d], tr.at[d], (tile, came)
        ).wait_recv()
    second = []
    for d in range(1, place.chips):
        copy = send(
            full.at[tile],
            full.at[tile],
            xs.at[d],
            xr.at[d],
            (place.chip_at(d) * 2 + place.core, time),
        )
        copy.start()
        second.append(copy)
    third = []
    for d in range(place.chips):
        came = place.chip_at(-d) * 2 + place.core
        if d:
            send(full.at[came], full.at[came], xs.at[d], xr.at[d], (came, time)).wait_recv()
        copy = send(
            full.at[came], full.at[came], ss.at[d], sr.at[d], (place.sibling, time)
        )
        copy.start()
        third.append(copy)
    for d in range(place.chips):
        came = place.chip_at(-d) * 2 + 1 - place.core
        send(
            full.at[came], full.at[came], ss.at[d], sr.at[d], (place.sibling, time)
        ).wait_recv()
    for copy in first + second + third:
        copy.wait_send()


def pair_sems(*counts):
    return [pltpu.SemaphoreType.DMA((n,)) for n in counts for _ in range(2)]


def pairs(sems):
    return [(sems[2 * k], sems[2 * k + 1]) for k in range(len(sems) // 2)]


def old_kernel(
    tiles, times, offsets_ref, weights_ref, old_ref, full_ref, sorted_ref, chunks, *sems
):
    place = Place(tiles, times)
    for i in range(times // 2):
        part = old_ref[:, i * LANES : (i + 1) * LANES].astype(jnp.float32)
        even, odd = chunks_of(part[:PACK], part[PACK:])
        chunks[2 * i] = even.astype(jnp.bfloat16)
        chunks[2 * i + 1] = odd.astype(jnp.bfloat16)
    place.greet()
    spread(
        place,
        chunks,
        full_ref,
        pairs(sems),
        lambda: sort_weights(offsets_ref, weights_ref, sorted_ref),
    )


def remote_params(identity, limit):
    return pltpu.CompilerParams(
        vmem_limit_bytes=limit * 2**20, collective_id=identity, has_side_effects=True
    )


def spread_old(traces_old, offsets, weights):
    tiles, times = lax.axis_size("tile"), lax.axis_size("tm")
    count, rows, cols = weights.shape
    return pl.pallas_call(
        functools.partial(old_kernel, tiles, times),
        out_shape=[
            jax.ShapeDtypeStruct((tiles, times * PACK, LANES), jnp.bfloat16),
            jax.ShapeDtypeStruct((count * PLANES, rows, cols // PLANES), jnp.float32),
        ],
        in_specs=[whole(SMEM), whole(), whole()],
        out_specs=[whole()] * 2,
        scratch_shapes=[pltpu.VMEM((times, PACK, LANES), jnp.bfloat16)]
        + pair_sems(times, tiles // 2, tiles // 2),
        compiler_params=remote_params(0, 12),
        name="spread_old",
    )(offsets, weights, traces_old)


def exchange_kernel(
    tiles, times, taps_ref, old_ref, sums_ref, full_ref, fresh_ref,
    pair_buf, x_send, x_buf, owner_send, owner_buf, stacked, spare, band, chunks, *sems
):
    place = Place(tiles, times)
    (ps, pr), (xs, xr), (ts, tr), *rest = pairs(sems)
    chips, tile, time, core = place.chips, place.tile, place.time, place.core
    rows = times * PACK
    place.greet()
    to_pair = []
    for d in [*range(1, chips), 0]:
        at = place.chip_at(d)
        copy = send(
            sums_ref.at[1 - core, at], pair_buf.at[at], ps.at[d], pr.at[d], (place.sibling, time)
        )
        copy.start()
        to_pair.append((d, at, copy))
    to_chip = []
    mine = None
    for d, at, copy in to_pair:
        copy.wait_recv()
        total = sums_ref[core, at].astype(jnp.float32) + pair_buf[at].astype(jnp.float32)
        if d:
            x_send[d] = total.astype(jnp.bfloat16)
            out = send(x_send.at[d], x_buf.at[d], xs.at[d], xr.at[d], (at * 2 + core, time))
            out.start()
            to_chip.append(out)
        else:
            mine = total
    for d, copy in enumerate(to_chip, 1):
        copy.wait_recv()
        mine += x_buf[d].astype(jnp.float32)
    owner_send[...] = mine[:rows].reshape(times, PACK, LANES)
    to_owner = []
    for d in range(1, times):
        peer = place.time_at(d)
        copy = send(owner_send.at[peer], owner_buf.at[time], ts.at[d], tr.at[d], (tile, peer))
        copy.start()
        to_owner.append(copy)
    owner_buf[time] = owner_send[time]

    spare[...] = jnp.zeros_like(spare)
    spare[0:1, 0 : taps_ref.shape[1]] = taps_ref[...]
    wide = jnp.broadcast_to(spare[0:1, :], (2 * LANES, 2 * LANES))
    band[...] = pltpu.roll(wide, LANES, 1, stride=1, stride_axis=0)[:, :LANES]

    high = mine[rows : rows + PACK]
    both = high + pltpu.roll(high, PACK - PACK // 2, 0)
    block = lax.rem(time * 2 * PACK, BLOCK)
    line = lax.broadcasted_iota(jnp.int32, (PACK, LANES), 0)
    lane = lax.broadcasted_iota(jnp.int32, (PACK, LANES), 1)
    row = jnp.sum(
        jnp.where(line == time // (BLOCK // (2 * PACK)), both, 0.0), axis=0, keepdims=True
    )
    columns = [
        jnp.sum(jnp.where(lane == line + block + k * PACK, row, 0.0), axis=1, keepdims=True)
        for k in range(2)
    ]
    divisor = jnp.where(lane < HALF_LANES, columns[0], columns[1]) + RIDGE

    for d in range(1, times):
        came = place.time_at(-d)
        send(
            owner_send.at[came], owner_buf.at[came], ts.at[d], tr.at[d], (tile, came)
        ).wait_recv()
    update = [jnp.zeros((PACK, LANES), jnp.float32)]
    for i in range(times // 2):
        part = old_ref[:, i * LANES : (i + 1) * LANES].astype(jnp.float32)
        for k, old in enumerate(chunks_of(part[:PACK], part[PACK:])):
            update.append(old + owner_buf[2 * i + k] / divisor)
    update.append(jnp.zeros((PACK, LANES), jnp.float32))
    steps = times // 2
    lines = [
        (join_low(update[2 * i], update[2 * i + 1]), join_high(update[2 * i], update[2 * i + 1]))
        for i in range(steps + 1)
    ]
    for i in range(steps):
        for k in range(2):
            at = slice((2 * i + k) * PACK, (2 * i + k + 1) * PACK)
            stacked[at, :LANES] = lines[i][k]
            stacked[at, LANES:] = lines[i + 1][k]
    made = jnp.dot(
        stacked[...],
        band[...],
        precision=lax.Precision.HIGHEST,
        preferred_element_type=jnp.float32,
    )
    made = jnp.maximum(made, 0.0)
    for i in range(steps):
        part = made[2 * i * PACK : (2 * i + 2) * PACK]
        fresh_ref[:, i * LANES : (i + 1) * LANES] = part.astype(jnp.bfloat16)
        even, odd = chunks_of(part[:PACK], part[PACK:])
        chunks[2 * i] = even.astype(jnp.bfloat16)
        chunks[2 * i + 1] = odd.astype(jnp.bfloat16)
    spread(place, chunks, full_ref, rest)
    for copy in [c for _, _, c in to_pair] + to_chip + to_owner:
        copy.wait_send()


def exchange(taps, traces_old, sums):
    tiles, times = lax.axis_size("tile"), lax.axis_size("tm")
    chips = tiles // 2
    rows = times * PACK
    group = (rows + PACK, LANES)
    return pl.pallas_call(
        functools.partial(exchange_kernel, tiles, times),
        out_shape=[
            jax.ShapeDtypeStruct((tiles, rows, LANES), jnp.bfloat16),
            jax.ShapeDtypeStruct(traces_old.shape, jnp.bfloat16),
        ],
        in_specs=[whole()] * 3,
        out_specs=[whole()] * 2,
        scratch_shapes=[
            pltpu.VMEM((chips,) + group, jnp.bfloat16),
            pltpu.VMEM((chips,) + group, jnp.bfloat16),
            pltpu.VMEM((chips,) + group, jnp.bfloat16),
            pltpu.VMEM((times, PACK, LANES), jnp.float32),
            pltpu.VMEM((times, PACK, LANES), jnp.float32),
            pltpu.VMEM((times * PACK, 2 * LANES), jnp.float32),
            pltpu.VMEM((8, 2 * LANES), jnp.float32),
            pltpu.VMEM((2 * LANES, LANES), jnp.float32),
            pltpu.VMEM((times, PACK, LANES), jnp.bfloat16),
        ]
        + pair_sems(chips, chips, times, times, chips, chips),
        compiler_params=remote_params(1, 12),
        name="exchange",
    )(taps[None, :], traces_old, sums)


PLANES = 2
REACH = RAD // PLANES
ROLLS = 2 * REACH + 1


def sorting(cols, back=False):
    column = lax.broadcasted_iota(jnp.int32, (cols, cols), int(back))
    place = lax.broadcasted_iota(jnp.int32, (cols, cols), 1 - int(back))
    half = cols // PLANES
    hit = column == PLANES * lax.rem(place, half) + place // half
    return hit.astype(jnp.float32).astype(jnp.bfloat16)


def sort_weights(offsets_ref, weights_ref, sorted_ref, each=8):
    count, rows, cols = weights_ref.shape
    sort = sorting(cols)
    column = lax.broadcasted_iota(jnp.int32, (rows, cols), 1)

    def some(step, carry):
        parts = []
        for u in range(each):
            j = step * each + u
            place = column + offsets_ref[1, j]
            parts.append(jnp.where((place >= 0) & (place < cols), weights_ref[j], 0.0))
        left = jnp.concatenate(parts, axis=0)
        total = jnp.zeros((each * rows, cols), jnp.float32)
        for _ in range(3):
            piece = left.astype(jnp.bfloat16)
            total += jnp.dot(piece, sort, preferred_element_type=jnp.float32)
            left = left - piece.astype(jnp.float32)
        for u in range(each):
            for p in range(PLANES):
                sorted_ref[(step * each + u) * PLANES + p] = total[
                    u * rows : (u + 1) * rows, p * LANES : (p + 1) * LANES
                ]
        return carry

    lax.fori_loop(0, count // each, some, 0)


def clean_kernel(
    tiles, offsets_ref, weights_ref, first_ref, third_ref, copies, field, halo, table, sends, recvs
):
    rows, frames, cols = first_ref.shape
    count = offsets_ref.shape[1]
    half = frames // 2
    padded = rows + 2 * RAD
    tile, time = lax.axis_index("tile"), lax.axis_index("tm")
    below, above = lax.rem(tile + 1, tiles), lax.rem(tile + tiles - 1, tiles)
    barrier = pltpu.get_barrier_semaphore()
    for peer in (below, above):
        pl.semaphore_signal(barrier, inc=1, device_id=(peer, time), device_id_type=MESH)

    sort = sorting(cols)

    def sort_rows(base):
        wide = jnp.dot(
            first_ref[pl.ds(base, RAD)].reshape(RAD * frames, cols),
            sort,
            preferred_element_type=jnp.float32,
        ).reshape(RAD, frames, cols)
        for p in range(PLANES):
            plane = wide[:, :, p * LANES : (p + 1) * LANES]
            field[0, pl.ds(base, RAD), p] = jnp.concatenate(
                [plane[:, :half], plane[:, half:]], axis=2
            ).astype(jnp.bfloat16)

    def halo_copies(turn):
        return [
            send(
                field.at[turn, pl.ds(start, RAD)],
                halo.at[turn, side],
                sends.at[turn, side],
                recvs.at[turn, side],
                (peer, time),
            )
            for side, start, peer in ((0, rows - RAD, below), (1, 0, above))
        ]

    def roll_row(values, row):
        for p in range(PLANES):
            wide = values[p]
            low, high = wide[:, :LANES], wide[:, LANES:]
            for s in range(ROLLS):
                shift = (REACH - s) % LANES
                at = (s * padded + row) * PLANES + p
                copies[at, :, :LANES] = pltpu.roll(low, shift, 1) if shift else low
                copies[at, :, LANES:] = pltpu.roll(high, shift, 1) if shift else high

    def roll_own(turn):
        def some(step, carry):
            for u in range(GROUP):
                row = step * GROUP + u
                roll_row(field[turn, row].astype(jnp.float32), RAD + row)
            return carry

        lax.fori_loop(0, rows // GROUP, some, 0)

    def roll_halo(turn):
        for side, edge, base in ((0, tile == 0, 0), (1, tile == tiles - 1, RAD + rows)):

            def some(step, carry, side=side, edge=edge, base=base):
                for u in range(GROUP):
                    row = step * GROUP + u
                    values = halo[turn, side, row].astype(jnp.float32)
                    roll_row(jnp.where(edge, 0.0, values), base + row)
                return carry

            lax.fori_loop(0, RAD // GROUP, some, 0)

    def run_rows(turn, edges):
        def one_row(step, carry):
            row = step + RAD
            if edges:
                row = jnp.where(step < RAD, step, step + rows - 2 * RAD)
            for p in range(PLANES):
                low = jnp.zeros((half, LANES), jnp.float32)
                high = jnp.zeros((half, LANES), jnp.float32)
                for j in range(count):
                    k = j * PLANES + p
                    source = copies[table[k] + row * PLANES]
                    weight = weights_ref[k, pl.ds(row, 1), :]
                    low += weight * source[:, :LANES]
                    high += weight * source[:, LANES:]
                mine = copies[(REACH * padded + RAD + row) * PLANES + p]
                out = mine - jnp.concatenate([low, high], axis=1)
                field[1 - turn, row, p] = out.astype(jnp.bfloat16)
            return carry

        lax.fori_loop(0, 2 * RAD if edges else rows - 2 * RAD, one_row, 0)

    sort_rows(0)
    sort_rows(rows - RAD)
    pl.semaphore_wait(barrier, 2)
    for turn in range(2):
        moving = halo_copies(turn)
        for copy in moving:
            copy.start()
        if turn == 0:
            for base in range(RAD, rows - RAD, RAD):
                sort_rows(base)
            for j in range(count):
                for p in range(PLANES):
                    q = p + offsets_ref[1, j] + RAD
                    table[j * PLANES + p] = (
                        (q >> 1) * padded + RAD + offsets_ref[0, j]
                    ) * PLANES + (q & 1)
        roll_own(turn)
        run_rows(turn, False)
        for copy in moving:
            copy.wait()
        roll_halo(turn)
        run_rows(turn, True)

    unsort = sorting(cols, back=True)
    for base in range(0, rows, RAD):
        planes = []
        for p in range(PLANES):
            wide = field[0, base : base + RAD, p].astype(jnp.float32)
            planes.append(jnp.concatenate([wide[:, :, :LANES], wide[:, :, LANES:]], axis=1))
        flat = jnp.concatenate(planes, axis=2).reshape(RAD * frames, cols)
        back = jnp.dot(flat.astype(jnp.bfloat16), unsort, preferred_element_type=jnp.float32)
        third_ref[base : base + RAD] = back.astype(jnp.bfloat16).reshape(RAD, frames, cols)


def clean(offsets, weights, first):
    rows, frames, cols = first.shape
    row = (PLANES, frames // 2, cols)
    padded = rows + 2 * RAD
    return pl.pallas_call(
        functools.partial(clean_kernel, lax.axis_size("tile")),
        out_shape=jax.ShapeDtypeStruct(first.shape, jnp.bfloat16),
        in_specs=[whole(SMEM), whole(), whole()],
        out_specs=whole(),
        scratch_shapes=[
            pltpu.VMEM((ROLLS * padded * PLANES,) + row[1:], jnp.float32),
            pltpu.VMEM((2, rows) + row, jnp.bfloat16),
            pltpu.VMEM((2, 2, RAD) + row, jnp.bfloat16),
            pltpu.SMEM((PLANES * offsets.shape[1],), jnp.int32),
            pltpu.SemaphoreType.DMA((2, 2)),
            pltpu.SemaphoreType.DMA((2, 2)),
        ],
        compiler_params=remote_params(2, 40),
        name="clean",
    )(offsets, weights, first)


def body(movie, footprints, support, cycle_offsets, cycle_weights, owner_map, traces_old, taps):
    tiles, slots = support.shape
    chips, times = lax.axis_size("tile") // 2, lax.axis_size("tm")
    foot = footprints.reshape(tiles, slots, TILE * TILE, BLOCK)
    field = movie.transpose(0, 2, 1)
    blocks, offsets = support.T, cycle_offsets.T
    old_full, weights = spread_old(traces_old, offsets, cycle_weights)
    old_full = old_full.reshape(-1, LANES)
    first = add_image(-1.0, blocks, owner_map, [old_full], foot, field, "first_residual")
    third = clean(offsets, weights, first)
    sums = project(blocks, owner_map, foot, third, chips, times)
    new_full, fresh = exchange(taps, traces_old, sums)
    new_full = new_full.reshape(-1, LANES)
    residual = add_image(
        1.0, blocks, owner_map, [old_full, new_full], foot, third, "final_residual"
    )
    return (residual.transpose(0, 2, 1), fresh)


def solution(mesh):
    return jax.shard_map(
        body,
        mesh=mesh,
        in_specs=(
            P("tile", None, "tm"),
            P("tile", None, None, None, None),
            P("tile", None),
            P(),
            P(None, "tile", None),
            P(),
            P(("tile", "tm"), None),
            P(),
        ),
        out_specs=(P("tile", None, "tm"), P(("tile", "tm"), None)),
        check_vma=False,
    )
```

```python
import functools
import math

import jax
import jax.numpy as jnp
from jax import lax
from jax.experimental import pallas as pl
from jax.experimental.pallas import tpu as pltpu
from jax.sharding import PartitionSpec as P

TILE = 32
BLOCK = 128
NBLK = 32
RAD = 8
RIDGE = 1.0
GROUP = 4
LANES = 128

SMEM = pltpu.MemorySpace.SMEM


def whole(space=pltpu.MemorySpace.VMEM):
    return pl.BlockSpec(memory_space=space)


def params(limit):
    return pltpu.CompilerParams(vmem_limit_bytes=limit * 2**20)


def cost(microseconds):
    return pl.CostEstimate(
        flops=microseconds * 10**9, bytes_accessed=microseconds * 10**6, transcendentals=0
    )


def block_of(support_ref, owner_ref, tile, slot):
    held = support_ref[slot, tile]
    return held >= 0, owner_ref[jnp.maximum(held, 0)]


def image_kernel(sign, both, support_ref, owner_ref, *refs):
    traces_refs, refs = refs[: 1 + both], refs[1 + both :]
    if both:
        foot_ref, field_ref, fresh_ref, out_ref, fresh_out, images = refs
        fresh_out[...] = fresh_ref[...]
    else:
        foot_ref, field_ref, out_ref, images = refs
    tiles, slots = foot_ref.shape[0], foot_ref.shape[1]
    rows, frames, cols = field_ref.shape
    group = LANES // TILE

    def block(tile, slot):
        live, position = block_of(support_ref, owner_ref, tile, slot)
        at = pl.ds(pl.multiple_of(position * (BLOCK // 2), BLOCK // 2), BLOCK // 2)
        if both:
            old, new = [ref[at, :].astype(jnp.float32) for ref in traces_refs]
            part = unpack(old - new)
        else:
            part = unpack(traces_refs[0][at, :])
        return jnp.where(live, part, jnp.zeros_like(part))

    for strip in range(cols // LANES):
        for inner in range(group):
            tile = strip * group + inner
            images[strip, :, inner * TILE : (inner + 1) * TILE, :] = jnp.dot(
                jnp.concatenate([foot_ref[tile, slot] for slot in range(slots)], axis=1),
                jnp.concatenate([block(tile, slot) for slot in range(slots)], axis=0),
                preferred_element_type=jnp.float32,
            ).reshape(rows, TILE, frames)
        lanes = slice(strip * LANES, (strip + 1) * LANES)
        for row in range(0, rows, 2):
            turned = jnp.concatenate([images[strip, row], images[strip, row + 1]], axis=1).T
            for k in range(2):
                part = turned[k * frames : (k + 1) * frames]
                out_ref[row + k, :, lanes] = (
                    field_ref[row + k, :, lanes].astype(jnp.float32) + sign * part
                ).astype(jnp.bfloat16)


def add_image(sign, support, owner_map, traces, foot, field, name, fresh=()):
    rows, frames, cols = field.shape
    made = pl.pallas_call(
        functools.partial(image_kernel, sign, len(traces) - 1),
        out_shape=[jax.ShapeDtypeStruct(x.shape, jnp.bfloat16) for x in (field, *fresh)],
        in_specs=[whole(SMEM), whole(SMEM)]
        + [whole() for _ in range(len(traces) + 2 + len(fresh))],
        out_specs=[whole() for _ in range(1 + len(fresh))],
        scratch_shapes=[pltpu.VMEM((cols // LANES, rows, LANES, frames), jnp.float32)],
        compiler_params=params(20),
        cost_estimate=cost(5),
        name=name,
    )(support, owner_map, *traces, foot, field, *fresh)
    return made if fresh else made[0]


def project_kernel(
    support_ref, owner_ref, foot_ref, field_ref, packed_ref, view, sums_ref, norms_ref
):
    tiles, slots, pixels, _ = foot_ref.shape
    rows, frames, cols = field_ref.shape
    group = LANES // TILE
    sums_ref[...] = jnp.zeros_like(sums_ref)
    norms_ref[...] = jnp.zeros_like(norms_ref)
    lane = lax.broadcasted_iota(jnp.int32, (frames, LANES), 1)

    def add(tile, slot):
        both = jnp.dot(
            view[tile],
            jnp.concatenate([foot_ref[tile, slot], foot_ref[tile, slot + 1]], axis=1),
            preferred_element_type=jnp.float32,
        )
        for k in range(2):
            live, position = block_of(support_ref, owner_ref, tile, slot + k)
            part = both[:, k * BLOCK : (k + 1) * BLOCK]
            sums_ref[position] += jnp.where(live, part, 0.0)
            wide = foot_ref[tile, slot + k].astype(jnp.float32)
            square = jnp.sum((wide * wide).reshape(pixels // 8, 8, BLOCK), axis=0)
            norms_ref[position] += jnp.where(live, square, 0.0)

    for strip in range(cols // LANES):
        lanes = slice(strip * LANES, (strip + 1) * LANES)

        for step in range(rows // group):
            source = [
                field_ref[step * group + k, :, lanes].astype(jnp.float32) for k in range(group)
            ]
            at = slice(step * LANES, (step + 1) * LANES)
            for t in range(group):
                line = None
                for k in range(group):
                    shift = (k - t) * TILE % LANES
                    moved = pltpu.roll(source[k], shift, 1) if shift else source[k]
                    line = moved if k == 0 else jnp.where(lane >= k * TILE, moved, line)
                view[strip * group + t, :, at] = line.astype(jnp.bfloat16)

        for inner in range(group):
            add(strip * group + inner, 0)

    for tile in range(tiles):
        for slot in range(2, slots, 2):

            @pl.when(support_ref[slot, tile] >= 0)
            def _(tile=tile, slot=slot):
                add(tile, slot)

    groups, each = packed_ref.shape[0], packed_ref.shape[1] - PACK
    per = each // frames
    for tile in range(groups):
        base = tile * per
        packed_ref[tile, :each] = (
            sums_ref[base : base + per].reshape(each, BLOCK).astype(jnp.bfloat16)
        )
        lines = [jnp.sum(norms_ref[base + q], axis=0, keepdims=True) for q in range(per)]
        fill = [jnp.zeros((PACK // 2 - per, BLOCK), jnp.float32)]
        norms = jnp.concatenate(lines + fill, axis=0)
        high = norms.astype(jnp.bfloat16).astype(jnp.float32)
        packed_ref[tile, each : each + PACK] = jnp.concatenate(
            [high, norms - high], axis=0
        ).astype(jnp.bfloat16)


def project(support, owner_map, foot, field, times):
    rows, frames, cols = field.shape
    return pl.pallas_call(
        project_kernel,
        out_shape=jax.ShapeDtypeStruct((lax.axis_size("tile"), times * PACK + PACK, LANES), jnp.bfloat16),
        in_specs=[whole(SMEM), whole(SMEM), whole(), whole()],
        out_specs=whole(),
        scratch_shapes=[
            pltpu.VMEM((foot.shape[0], frames, TILE * TILE), jnp.bfloat16),
            pltpu.VMEM((NBLK, frames, BLOCK), jnp.float32),
            pltpu.VMEM((NBLK, 8, BLOCK), jnp.float32),
        ],
        compiler_params=params(20),
        cost_estimate=cost(7),
        name="project",
    )(support, owner_map, foot, field)


MESH = pl.DeviceIdType.MESH
PACK = 16
HALF_LANES = LANES // 2


def low_lanes():
    return lax.broadcasted_iota(jnp.int32, (PACK, LANES), 1) < HALF_LANES


def join_low(left, right):
    return jnp.where(low_lanes(), left, pltpu.roll(right, HALF_LANES, 1))


def join_high(left, right):
    return jnp.where(low_lanes(), pltpu.roll(left, HALF_LANES, 1), right)


def chunks_of(top, bottom):
    return join_low(top, bottom), join_high(top, bottom)


def unpack(packed):
    wide = packed.astype(jnp.float32)
    turned = pltpu.roll(wide, HALF_LANES, 1)
    parts = []
    for k in range(packed.shape[0] // PACK):
        rows = slice(k * PACK, (k + 1) * PACK)
        parts += [wide[rows, :HALF_LANES], turned[rows, :HALF_LANES]]
    return jnp.concatenate(parts, axis=0).astype(jnp.bfloat16)


def far_first(peers, square):
    side = math.isqrt(peers) if square else peers
    if square and side * side != peers:
        side = peers
    steps = [(a, b) for a in range(peers // side) for b in range(side)][1:]

    def hops(step):
        return min(step[0], peers // side - step[0]) + min(step[1], side - step[1])

    return side, sorted(steps, key=hops, reverse=True)


class Place:
    def __init__(self, tiles, times):
        self.chips, self.times = tiles // 2, times
        self.tile, self.time = lax.axis_index("tile"), lax.axis_index("tm")
        self.chip, self.core = self.tile // 2, lax.rem(self.tile, 2)
        self.side, self.time_steps = far_first(times, True)
        chip_steps = [b for _, b in far_first(self.chips, False)[1]]
        self.tile_steps = [(b, k) for b in chip_steps for k in range(2)] + [(0, 1)]

    def tile_at(self, step, sign=1):
        core = 1 - self.core if step[1] else self.core
        return lax.rem(self.chip + sign * step[0] + self.chips, self.chips) * 2 + core

    def time_at(self, d, sign=1):
        a, b = self.time_steps[d - 1]
        rings = self.times // self.side
        return lax.rem(self.time // self.side + sign * a + rings, rings) * self.side + lax.rem(
            lax.rem(self.time, self.side) + sign * b + self.side, self.side
        )

    def signal(self):
        barrier = pltpu.get_barrier_semaphore()
        peers = [(self.tile, self.time_at(d)) for d in range(1, self.times)]
        peers += [(self.tile_at(step), self.time) for step in self.tile_steps]
        for peer in peers:
            pl.semaphore_signal(barrier, inc=1, device_id=peer, device_id_type=MESH)
        self.peers = len(peers)

    def wait(self):
        pl.semaphore_wait(pltpu.get_barrier_semaphore(), self.peers)


def send(source, target, send_sem, recv_sem, device):
    return pltpu.make_async_remote_copy(
        src_ref=source,
        dst_ref=target,
        send_sem=send_sem,
        recv_sem=recv_sem,
        device_id=device,
        device_id_type=MESH,
    )


def spread(place, chunks, full, sems, meanwhile=None):
    (ts, tr), (xs, xr) = sems
    tile, time = place.tile, place.time

    def rows(index):
        return pl.ds(pl.multiple_of(index * PACK, PACK), PACK)

    first = []
    for d in range(1, place.times):
        peer = place.time_at(d)
        copy = send(
            chunks.at[peer], full.at[tile, rows(time)], ts.at[d], tr.at[d], (tile, peer)
        )
        copy.start()
        first.append(copy)
    full[tile, rows(time)] = chunks[time]
    if meanwhile:
        meanwhile()
    for d, copy in enumerate(first, 1):
        came = place.time_at(d, -1)
        send(
            chunks.at[time], full.at[tile, rows(came)], ts.at[d], tr.at[d], (tile, came)
        ).wait_recv()
    second = []
    for i, step in enumerate(place.tile_steps):
        copy = send(
            full.at[tile], full.at[tile], xs.at[i], xr.at[i], (place.tile_at(step), time)
        )
        copy.start()
        second.append(copy)
    for i, step in enumerate(place.tile_steps):
        came = place.tile_at(step, -1)
        send(full.at[came], full.at[came], xs.at[i], xr.at[i], (came, time)).wait_recv()
    for copy in first + second:
        copy.wait_send()


def pair_sems(*counts):
    return [pltpu.SemaphoreType.DMA((n,)) for n in counts for _ in range(2)]


def pairs(sems):
    return [(sems[2 * k], sems[2 * k + 1]) for k in range(len(sems) // 2)]


def old_kernel(
    tiles, times, offsets_ref, weights_hbm, old_hbm, full_ref, sorted_ref,
    weights, old, chunks, local, *sems
):
    place = Place(tiles, times)
    fetch_old = pltpu.make_async_copy(old_hbm, old, local.at[0])
    fetch_old.start()
    fetch_weights = pltpu.make_async_copy(weights_hbm, weights, local.at[1])
    fetch_weights.start()
    place.signal()
    fetch_old.wait()
    for i in range(times // 2):
        part = old[:, i * LANES : (i + 1) * LANES].astype(jnp.float32)
        even, odd = chunks_of(part[:PACK], part[PACK:])
        chunks[2 * i] = even.astype(jnp.bfloat16)
        chunks[2 * i + 1] = odd.astype(jnp.bfloat16)
    place.wait()

    def meanwhile():
        fetch_weights.wait()
        sort_weights(offsets_ref, weights, sorted_ref)

    spread(place, chunks, full_ref, pairs(sems), meanwhile)


def remote_params(identity, limit):
    return pltpu.CompilerParams(
        vmem_limit_bytes=limit * 2**20, collective_id=identity, has_side_effects=True
    )


def spread_old(traces_old, offsets, weights):
    tiles, times = lax.axis_size("tile"), lax.axis_size("tm")
    count, rows, cols = weights.shape
    return pl.pallas_call(
        functools.partial(old_kernel, tiles, times),
        out_shape=[
            jax.ShapeDtypeStruct((tiles, times * PACK, LANES), jnp.bfloat16),
            jax.ShapeDtypeStruct((count * PLANES, rows, LANES), jnp.float32),
        ],
        in_specs=[whole(SMEM), whole(pltpu.MemorySpace.HBM), whole(pltpu.MemorySpace.HBM)],
        out_specs=[whole()] * 2,
        scratch_shapes=[
            pltpu.VMEM(weights.shape, weights.dtype),
            pltpu.VMEM(traces_old.shape, traces_old.dtype),
            pltpu.VMEM((times, PACK, LANES), jnp.bfloat16),
            pltpu.SemaphoreType.DMA((2,)),
        ]
        + pair_sems(times, tiles - 1),
        compiler_params=remote_params(0, 54),
        cost_estimate=cost(15),
        name="spread_old",
    )(offsets, weights, traces_old)


def exchange_kernel(
    tiles, times, taps_ref, old_ref, sums_ref, full_ref, fresh_ref,
    group_buf, owner_send, owner_buf, stacked, spare, band, chunks, *sems
):
    place = Place(tiles, times)
    (gs, gr), (ts, tr), *rest = pairs(sems)
    tile, time = place.tile, place.time
    rows = times * PACK
    place.signal()
    place.wait()
    to_group = []
    for i, step in enumerate(place.tile_steps):
        peer = place.tile_at(step)
        copy = send(sums_ref.at[peer], group_buf.at[i], gs.at[i], gr.at[i], (peer, time))
        copy.start()
        to_group.append(copy)
    mine = sums_ref[tile].astype(jnp.float32)
    for i, copy in reversed(list(enumerate(to_group))):
        copy.wait_recv()
        mine += group_buf[i].astype(jnp.float32)
    frames = rows * LANES // (2 * PACK * times)
    each = BLOCK // (2 * PACK)
    for q in range(rows // frames):
        turned = mine[q * frames : (q + 1) * frames].T
        for k in range(each):
            top = turned[2 * k * PACK : (2 * k + 1) * PACK]
            bottom = turned[(2 * k + 1) * PACK : (2 * k + 2) * PACK]
            owner_send[q * each + k] = jnp.concatenate([top, bottom], axis=1)
    to_owner = []
    for d in range(1, times):
        peer = place.time_at(d)
        copy = send(owner_send.at[peer], owner_buf.at[time], ts.at[d], tr.at[d], (tile, peer))
        copy.start()
        to_owner.append(copy)
    owner_buf[time] = owner_send[time]

    spare[...] = jnp.zeros_like(spare)
    spare[0:1, 0 : taps_ref.shape[1]] = taps_ref[...]
    wide = jnp.broadcast_to(spare[0:1, :], (2 * LANES, 2 * LANES))
    band[...] = pltpu.roll(wide, LANES, 1, stride=1, stride_axis=0)[:, :LANES]

    high = mine[rows : rows + PACK]
    both = high + pltpu.roll(high, PACK - PACK // 2, 0)
    block = lax.rem(time * 2 * PACK, BLOCK)
    line = lax.broadcasted_iota(jnp.int32, (PACK, LANES), 0)
    lane = lax.broadcasted_iota(jnp.int32, (PACK, LANES), 1)
    row = jnp.sum(
        jnp.where(line == time // (BLOCK // (2 * PACK)), both, 0.0), axis=0, keepdims=True
    )
    columns = [
        jnp.sum(jnp.where(lane == line + block + k * PACK, row, 0.0), axis=1, keepdims=True)
        for k in range(2)
    ]
    divisor = jnp.where(lane < HALF_LANES, columns[0], columns[1]) + RIDGE

    for d in range(1, times):
        came = place.time_at(d, -1)
        send(
            owner_send.at[came], owner_buf.at[came], ts.at[d], tr.at[d], (tile, came)
        ).wait_recv()
    update = [jnp.zeros((PACK, LANES), jnp.float32)]
    for i in range(times // 2):
        part = old_ref[:, i * LANES : (i + 1) * LANES].astype(jnp.float32)
        for k, old in enumerate(chunks_of(part[:PACK], part[PACK:])):
            update.append(old + owner_buf[2 * i + k] / divisor)
    update.append(jnp.zeros((PACK, LANES), jnp.float32))
    steps = times // 2
    lines = [
        (join_low(update[2 * i], update[2 * i + 1]), join_high(update[2 * i], update[2 * i + 1]))
        for i in range(steps + 1)
    ]
    for i in range(steps):
        for k in range(2):
            at = slice((2 * i + k) * PACK, (2 * i + k + 1) * PACK)
            stacked[at, :LANES] = lines[i][k]
            stacked[at, LANES:] = lines[i + 1][k]
    made = jnp.dot(
        stacked[...],
        band[...],
        precision=lax.Precision.HIGHEST,
        preferred_element_type=jnp.float32,
    )
    made = jnp.maximum(made, 0.0)
    for i in range(steps):
        part = made[2 * i * PACK : (2 * i + 2) * PACK]
        fresh_ref[:, i * LANES : (i + 1) * LANES] = part.astype(jnp.bfloat16)
        even, odd = chunks_of(part[:PACK], part[PACK:])
        chunks[2 * i] = even.astype(jnp.bfloat16)
        chunks[2 * i + 1] = odd.astype(jnp.bfloat16)
    spread(place, chunks, full_ref, rest)
    for copy in to_group + to_owner:
        copy.wait_send()


def exchange(taps, traces_old, sums):
    tiles, times = lax.axis_size("tile"), lax.axis_size("tm")
    rows = times * PACK
    return pl.pallas_call(
        functools.partial(exchange_kernel, tiles, times),
        out_shape=[
            jax.ShapeDtypeStruct((tiles, rows, LANES), jnp.bfloat16),
            jax.ShapeDtypeStruct(traces_old.shape, jnp.bfloat16),
        ],
        in_specs=[whole()] * 3,
        out_specs=[whole()] * 2,
        scratch_shapes=[
            pltpu.VMEM((tiles - 1, rows + PACK, LANES), jnp.bfloat16),
            pltpu.VMEM((times, PACK, LANES), jnp.float32),
            pltpu.VMEM((times, PACK, LANES), jnp.float32),
            pltpu.VMEM((times * PACK, 2 * LANES), jnp.float32),
            pltpu.VMEM((8, 2 * LANES), jnp.float32),
            pltpu.VMEM((2 * LANES, LANES), jnp.float32),
            pltpu.VMEM((times, PACK, LANES), jnp.bfloat16),
        ]
        + pair_sems(tiles - 1, times, times, tiles - 1),
        compiler_params=remote_params(1, 12),
        cost_estimate=cost(25),
        name="exchange",
    )(taps[None, :], traces_old, sums)


PLANES = 4
REACH = RAD // PLANES
ROLLS = 2 * REACH + 1


def sorting(cols):
    shape = (cols, PLANES * LANES)
    column = lax.broadcasted_iota(jnp.int32, shape, 0)
    place = lax.broadcasted_iota(jnp.int32, shape, 1)
    hit = column == PLANES * lax.rem(place, LANES // 2) + place // LANES
    return hit.astype(jnp.float32).astype(jnp.bfloat16)


def unsorting(cols):
    shape = (PLANES * LANES, 2 * cols)
    place = lax.broadcasted_iota(jnp.int32, shape, 0)
    target = lax.broadcasted_iota(jnp.int32, shape, 1)
    hit = target == lax.rem(place, LANES) // (LANES // 2) * cols + (
        PLANES * lax.rem(place, LANES // 2) + place // LANES
    )
    return hit.astype(jnp.float32).astype(jnp.bfloat16)


def sort_weights(offsets_ref, weights_ref, sorted_ref, each=8):
    count, rows, cols = weights_ref.shape
    sort = sorting(cols)
    column = lax.broadcasted_iota(jnp.int32, (rows, cols), 1)

    def some(step, carry):
        parts = []
        for u in range(each):
            j = step * each + u
            place = column + offsets_ref[1, j]
            parts.append(jnp.where((place >= 0) & (place < cols), weights_ref[j], 0.0))
        left = jnp.concatenate(parts, axis=0)
        total = jnp.zeros((each * rows, PLANES * LANES), jnp.float32)
        for _ in range(3):
            piece = left.astype(jnp.bfloat16)
            total += jnp.dot(piece, sort, preferred_element_type=jnp.float32)
            left = left - piece.astype(jnp.float32)
        for u in range(each):
            for p in range(PLANES):
                sorted_ref[(step * each + u) * PLANES + p] = total[
                    u * rows : (u + 1) * rows, p * LANES : (p + 1) * LANES
                ]
        return carry

    lax.fori_loop(0, count // each, some, 0)


def clean_kernel(
    tiles, offsets_ref, weights_ref, first_ref, third_ref,
    copies_0, copies_1, field, halo, table, sends, recvs
):
    rows, frames, cols = first_ref.shape
    count = offsets_ref.shape[1]
    half = frames // 2
    padded = rows + 2 * RAD
    copies = (copies_0, copies_1)
    tile, time = lax.axis_index("tile"), lax.axis_index("tm")
    below, above = lax.rem(tile + 1, tiles), lax.rem(tile + tiles - 1, tiles)
    barrier = pltpu.get_barrier_semaphore()
    for peer in (below, above):
        pl.semaphore_signal(barrier, inc=1, device_id=(peer, time), device_id_type=MESH)

    sort = sorting(cols)
    lower = lax.broadcasted_iota(jnp.int32, (RAD, half, LANES), 2) < LANES // 2

    def sort_rows(base):
        wide = jnp.dot(
            first_ref[pl.ds(base, RAD)].reshape(RAD * frames, cols),
            sort,
            preferred_element_type=jnp.float32,
        ).reshape(RAD, frames, PLANES * LANES)
        for p in range(PLANES):
            plane = wide[:, :, p * LANES : (p + 1) * LANES]
            field[0, pl.ds(base, RAD), p] = jnp.where(
                lower, plane[:, :half], plane[:, half:]
            ).astype(jnp.bfloat16)

    def halo_copies(turn):
        return [
            send(
                field.at[turn, pl.ds(start, RAD)],
                halo.at[turn, side],
                sends.at[turn, side],
                recvs.at[turn, side],
                (peer, time),
            )
            for side, start, peer in ((0, rows - RAD, below), (1, 0, above))
        ]

    def roll_plane(turn, p, values, row):
        for s in range(ROLLS):
            shift = (REACH - s) % LANES
            copies[turn][(s * PLANES + p) * padded + row] = (
                pltpu.roll(values, shift, 1) if shift else values
            )

    def roll_own():
        def some(step, carry):
            for u in range(2 * RAD):
                row = step * 2 * RAD + u
                for p in range(PLANES):
                    roll_plane(0, p, field[0, row, p].astype(jnp.float32), RAD + row)
            return carry

        lax.fori_loop(0, rows // (2 * RAD), some, 0)

    def roll_halo(turn):
        for side, edge, base in ((0, tile == 0, 0), (1, tile == tiles - 1, RAD + rows)):
            for row in range(RAD):
                for p in range(PLANES):
                    values = halo[turn, side, row, p].astype(jnp.float32)
                    roll_plane(turn, p, jnp.where(edge, 0.0, values), base + row)

    def run_rows(turn, edges):
        def some(step, carry):
            row = step * RAD + RAD
            if edges:
                row = jnp.where(step < RAD // RAD, step * RAD, step * RAD + rows - 2 * RAD)
            for p in range(PLANES):
                total = [jnp.zeros((half, LANES), jnp.float32) for _ in range(RAD)]
                for j in range(count):
                    k = j * PLANES + p
                    source = copies[turn][pl.ds(table[k] + row, RAD)]
                    for r in range(RAD):
                        total[r] += weights_ref[k, pl.ds(row + r, 1), :] * source[r]
                mine = copies[turn][pl.ds((REACH * PLANES + p) * padded + RAD + row, RAD)]
                for r in range(RAD):
                    out = (mine[r] - total[r]).astype(jnp.bfloat16)
                    field[1 - turn, row + r, p] = out
                    if turn == 0:
                        roll_plane(1, p, out.astype(jnp.float32), RAD + row + r)
            return carry

        lax.fori_loop(0, (2 * RAD if edges else rows - 2 * RAD) // RAD, some, 0)

    sort_rows(0)
    sort_rows(rows - RAD)
    pl.semaphore_wait(barrier, 2)
    for turn in range(2):
        moving = halo_copies(turn)
        for copy in moving:
            copy.start()
        if turn == 0:
            for base in range(RAD, rows - RAD, RAD):
                sort_rows(base)
            for j in range(count):
                for p in range(PLANES):
                    q = p + offsets_ref[1, j] + RAD
                    table[j * PLANES + p] = q * padded + RAD + offsets_ref[0, j]
            roll_own()
        run_rows(turn, False)
        for copy in moving:
            copy.wait()
        roll_halo(turn)
        run_rows(turn, True)

    unsort = unsorting(cols)
    for base in range(0, rows, RAD):
        planes = [field[0, base : base + RAD, p].astype(jnp.float32) for p in range(PLANES)]
        flat = jnp.concatenate(planes, axis=2).reshape(RAD * half, PLANES * LANES)
        back = jnp.dot(flat.astype(jnp.bfloat16), unsort, preferred_element_type=jnp.float32)
        back = back.astype(jnp.bfloat16).reshape(RAD, half, 2 * cols)
        for k in range(2):
            third_ref[base : base + RAD, k * half : (k + 1) * half] = back[
                :, :, k * cols : (k + 1) * cols
            ]


def clean(offsets, weights, first):
    rows, frames, cols = first.shape
    row = (PLANES, frames // 2, LANES)
    copies = pltpu.VMEM((ROLLS * PLANES * (rows + 2 * RAD),) + row[1:], jnp.float32)
    return pl.pallas_call(
        functools.partial(clean_kernel, lax.axis_size("tile")),
        out_shape=jax.ShapeDtypeStruct(first.shape, jnp.bfloat16),
        in_specs=[whole(SMEM), whole(), whole()],
        out_specs=whole(),
        scratch_shapes=[
            copies,
            copies,
            pltpu.VMEM((2, rows) + row, jnp.bfloat16),
            pltpu.VMEM((2, 2, RAD) + row, jnp.bfloat16),
            pltpu.SMEM((PLANES * offsets.shape[1],), jnp.int32),
            pltpu.SemaphoreType.DMA((2, 2)),
            pltpu.SemaphoreType.DMA((2, 2)),
        ],
        compiler_params=remote_params(2, 42),
        cost_estimate=cost(25),
        name="clean",
    )(offsets, weights, first)


def body(movie, footprints, support, cycle_offsets, cycle_weights, owner_map, traces_old, taps):
    tiles, slots = support.shape
    times = lax.axis_size("tm")
    foot = footprints.reshape(tiles, slots, TILE * TILE, BLOCK)
    field = movie.transpose(0, 2, 1)
    blocks, offsets = support.T, cycle_offsets.T
    old_full, weights = spread_old(traces_old, offsets, cycle_weights)
    old_full = old_full.reshape(-1, LANES)
    first = add_image(-1.0, blocks, owner_map, [old_full], foot, field, "first_residual")
    third = clean(offsets, weights, first)
    sums = project(blocks, owner_map, foot, third, times)
    new_full, fresh = exchange(taps, traces_old, sums)
    new_full = new_full.reshape(-1, LANES)
    residual, fresh = add_image(
        1.0, blocks, owner_map, [old_full, new_full], foot, third, "final_residual", (fresh,)
    )
    return (residual.transpose(0, 2, 1), fresh)


def solution(mesh):
    return jax.shard_map(
        body,
        mesh=mesh,
        in_specs=(
            P("tile", None, "tm"),
            P("tile", None, None, None, None),
            P("tile", None),
            P(),
            P(None, "tile", None),
            P(),
            P(("tile", "tm"), None),
            P(),
        ),
        out_specs=(P("tile", None, "tm"), P(("tile", "tm"), None)),
        check_vma=False,
    )
```

```python
import functools
import math

import jax
import jax.numpy as jnp
from jax import lax
from jax.experimental import pallas as pl
from jax.experimental.pallas import tpu as pltpu
from jax.sharding import PartitionSpec as P

TILE = 32
BLOCK = 128
NBLK = 32
RAD = 8
RIDGE = 1.0
GROUP = 4
LANES = 128

SMEM = pltpu.MemorySpace.SMEM


def whole(space=pltpu.MemorySpace.VMEM):
    return pl.BlockSpec(memory_space=space)


def params(limit):
    return pltpu.CompilerParams(vmem_limit_bytes=limit * 2**20)


def cost(microseconds):
    return pl.CostEstimate(
        flops=microseconds * 10**9, bytes_accessed=microseconds * 10**6, transcendentals=0
    )


def block_of(support_ref, owner_ref, tile, slot):
    held = support_ref[slot, tile]
    return held >= 0, owner_ref[jnp.maximum(held, 0)]


def image_kernel(sign, both, support_ref, owner_ref, *refs):
    traces_refs, refs = refs[: 1 + both], refs[1 + both :]
    if both:
        foot_ref, field_ref, fresh_ref, out_ref, fresh_out, images = refs
        fresh_out[...] = fresh_ref[...]
    else:
        foot_ref, field_ref, out_ref, images = refs
    tiles, slots = foot_ref.shape[0], foot_ref.shape[1]
    rows, frames, cols = field_ref.shape
    group = LANES // TILE

    def block(tile, slot):
        live, position = block_of(support_ref, owner_ref, tile, slot)
        at = pl.ds(pl.multiple_of(position * (BLOCK // 2), BLOCK // 2), BLOCK // 2)
        if both:
            old, new = [ref[at, :].astype(jnp.float32) for ref in traces_refs]
            part = unpack(old - new)
        else:
            part = unpack(traces_refs[0][at, :])
        return jnp.where(live, part, jnp.zeros_like(part))

    for strip in range(cols // LANES):
        for inner in range(group):
            tile = strip * group + inner
            images[strip, :, inner * TILE : (inner + 1) * TILE, :] = jnp.dot(
                jnp.concatenate([foot_ref[tile, slot] for slot in range(slots)], axis=1),
                jnp.concatenate([block(tile, slot) for slot in range(slots)], axis=0),
                preferred_element_type=jnp.float32,
            ).reshape(rows, TILE, frames)
        lanes = slice(strip * LANES, (strip + 1) * LANES)
        for row in range(0, rows, 2):
            turned = jnp.concatenate([images[strip, row], images[strip, row + 1]], axis=1).T
            for k in range(2):
                part = turned[k * frames : (k + 1) * frames]
                out_ref[row + k, :, lanes] = (
                    field_ref[row + k, :, lanes].astype(jnp.float32) + sign * part
                ).astype(jnp.bfloat16)


def add_image(sign, support, owner_map, traces, foot, field, name, fresh=()):
    rows, frames, cols = field.shape
    made = pl.pallas_call(
        functools.partial(image_kernel, sign, len(traces) - 1),
        out_shape=[jax.ShapeDtypeStruct(x.shape, jnp.bfloat16) for x in (field, *fresh)],
        in_specs=[whole(SMEM), whole(SMEM)]
        + [whole() for _ in range(len(traces) + 2 + len(fresh))],
        out_specs=[whole() for _ in range(1 + len(fresh))],
        scratch_shapes=[pltpu.VMEM((cols // LANES, rows, LANES, frames), jnp.float32)],
        compiler_params=params(20),
        cost_estimate=cost(5),
        name=name,
    )(support, owner_map, *traces, foot, field, *fresh)
    return made if fresh else made[0]


def project_kernel(
    support_ref, owner_ref, foot_ref, field_ref, packed_ref, view, sums_ref, norms_ref
):
    tiles, slots, pixels, _ = foot_ref.shape
    rows, frames, cols = field_ref.shape
    group = LANES // TILE
    sums_ref[...] = jnp.zeros_like(sums_ref)
    norms_ref[...] = jnp.zeros_like(norms_ref)
    lane = lax.broadcasted_iota(jnp.int32, (frames, LANES), 1)

    def add(tile, slot):
        both = jnp.dot(
            view[tile],
            jnp.concatenate([foot_ref[tile, slot], foot_ref[tile, slot + 1]], axis=1),
            preferred_element_type=jnp.float32,
        )
        for k in range(2):
            live, position = block_of(support_ref, owner_ref, tile, slot + k)
            part = both[:, k * BLOCK : (k + 1) * BLOCK]
            sums_ref[position] += jnp.where(live, part, 0.0)
            wide = foot_ref[tile, slot + k].astype(jnp.float32)
            square = jnp.sum((wide * wide).reshape(pixels // 8, 8, BLOCK), axis=0)
            norms_ref[position] += jnp.where(live, square, 0.0)

    for strip in range(cols // LANES):
        lanes = slice(strip * LANES, (strip + 1) * LANES)

        for step in range(rows // group):
            source = [
                field_ref[step * group + k, :, lanes].astype(jnp.float32) for k in range(group)
            ]
            at = slice(step * LANES, (step + 1) * LANES)
            for t in range(group):
                line = None
                for k in range(group):
                    shift = (k - t) * TILE % LANES
                    moved = pltpu.roll(source[k], shift, 1) if shift else source[k]
                    line = moved if k == 0 else jnp.where(lane >= k * TILE, moved, line)
                view[strip * group + t, :, at] = line.astype(jnp.bfloat16)

        for inner in range(group):
            add(strip * group + inner, 0)

    for tile in range(tiles):
        for slot in range(2, slots, 2):

            @pl.when(support_ref[slot, tile] >= 0)
            def _(tile=tile, slot=slot):
                add(tile, slot)

    each = packed_ref.shape[2] - PACK
    per = each // frames
    for core in range(packed_ref.shape[0]):
        for chip in range(packed_ref.shape[1]):
            base = (2 * chip + core) * per
            packed_ref[core, chip, :each] = (
                sums_ref[base : base + per].reshape(each, BLOCK).astype(jnp.bfloat16)
            )
            lines = [jnp.sum(norms_ref[base + q], axis=0, keepdims=True) for q in range(per)]
            fill = [jnp.zeros((PACK // 2 - per, BLOCK), jnp.float32)]
            norms = jnp.concatenate(lines + fill, axis=0)
            high = norms.astype(jnp.bfloat16).astype(jnp.float32)
            packed_ref[core, chip, each : each + PACK] = jnp.concatenate(
                [high, norms - high], axis=0
            ).astype(jnp.bfloat16)


def project(support, owner_map, foot, field, chips, times):
    rows, frames, cols = field.shape
    return pl.pallas_call(
        project_kernel,
        out_shape=jax.ShapeDtypeStruct((2, chips, times * PACK + PACK, LANES), jnp.bfloat16),
        in_specs=[whole(SMEM), whole(SMEM), whole(), whole()],
        out_specs=whole(),
        scratch_shapes=[
            pltpu.VMEM((foot.shape[0], frames, TILE * TILE), jnp.bfloat16),
            pltpu.VMEM((NBLK, frames, BLOCK), jnp.float32),
            pltpu.VMEM((NBLK, 8, BLOCK), jnp.float32),
        ],
        compiler_params=params(20),
        cost_estimate=cost(7),
        name="project",
    )(support, owner_map, foot, field)


MESH = pl.DeviceIdType.MESH
PACK = 16
HALF_LANES = LANES // 2


def low_lanes():
    return lax.broadcasted_iota(jnp.int32, (PACK, LANES), 1) < HALF_LANES


def join_low(left, right):
    return jnp.where(low_lanes(), left, pltpu.roll(right, HALF_LANES, 1))


def join_high(left, right):
    return jnp.where(low_lanes(), pltpu.roll(left, HALF_LANES, 1), right)


def chunks_of(top, bottom):
    return join_low(top, bottom), join_high(top, bottom)


def unpack(packed):
    wide = packed.astype(jnp.float32)
    turned = pltpu.roll(wide, HALF_LANES, 1)
    parts = []
    for k in range(packed.shape[0] // PACK):
        rows = slice(k * PACK, (k + 1) * PACK)
        parts += [wide[rows, :HALF_LANES], turned[rows, :HALF_LANES]]
    return jnp.concatenate(parts, axis=0).astype(jnp.bfloat16)


def far_first(peers, square):
    side = math.isqrt(peers) if square else peers
    if square and side * side != peers:
        side = peers
    steps = [(a, b) for a in range(peers // side) for b in range(side)][1:]

    def hops(step):
        return min(step[0], peers // side - step[0]) + min(step[1], side - step[1])

    return side, sorted(steps, key=hops, reverse=True)


class Place:
    def __init__(self, tiles, times):
        self.chips, self.times = tiles // 2, times
        self.tile, self.time = lax.axis_index("tile"), lax.axis_index("tm")
        self.chip, self.core = self.tile // 2, lax.rem(self.tile, 2)
        self.sibling = self.chip * 2 + 1 - self.core
        self.side, self.time_steps = far_first(times, True)
        self.chip_steps = [b for _, b in far_first(self.chips, False)[1]]

    def chip_at(self, step):
        return lax.rem(self.chip + step + self.chips, self.chips)

    def time_at(self, d, sign=1):
        a, b = self.time_steps[d - 1]
        rings = self.times // self.side
        return lax.rem(self.time // self.side + sign * a + rings, rings) * self.side + lax.rem(
            lax.rem(self.time, self.side) + sign * b + self.side, self.side
        )

    def signal(self):
        barrier = pltpu.get_barrier_semaphore()
        peers = [(self.tile, self.time_at(d)) for d in range(1, self.times)]
        peers += [(self.chip_at(d) * 2 + self.core, self.time) for d in self.chip_steps]
        peers += [(self.sibling, self.time)]
        for peer in peers:
            pl.semaphore_signal(barrier, inc=1, device_id=peer, device_id_type=MESH)
        self.peers = len(peers)

    def wait(self):
        pl.semaphore_wait(pltpu.get_barrier_semaphore(), self.peers)


def send(source, target, send_sem, recv_sem, device):
    return pltpu.make_async_remote_copy(
        src_ref=source,
        dst_ref=target,
        send_sem=send_sem,
        recv_sem=recv_sem,
        device_id=device,
        device_id_type=MESH,
    )


def spread(place, chunks, full, sems, meanwhile=None):
    (ts, tr), (xs, xr), (ss, sr) = sems
    tile, time = place.tile, place.time

    def rows(index):
        return pl.ds(pl.multiple_of(index * PACK, PACK), PACK)

    first = []
    for d in range(1, place.times):
        peer = place.time_at(d)
        copy = send(
            chunks.at[peer], full.at[tile, rows(time)], ts.at[d], tr.at[d], (tile, peer)
        )
        copy.start()
        first.append(copy)
    full[tile, rows(time)] = chunks[time]
    if meanwhile:
        meanwhile()
    for d, copy in enumerate(first, 1):
        came = place.time_at(d, -1)
        send(
            chunks.at[time], full.at[tile, rows(came)], ts.at[d], tr.at[d], (tile, came)
        ).wait_recv()
    second = []
    for d in place.chip_steps:
        copy = send(
            full.at[tile],
            full.at[tile],
            xs.at[d],
            xr.at[d],
            (place.chip_at(d) * 2 + place.core, time),
        )
        copy.start()
        second.append(copy)
    third = []
    for d in [0, *reversed(place.chip_steps)]:
        came = place.chip_at(-d) * 2 + place.core
        if d:
            send(full.at[came], full.at[came], xs.at[d], xr.at[d], (came, time)).wait_recv()
        copy = send(
            full.at[came], full.at[came], ss.at[d], sr.at[d], (place.sibling, time)
        )
        copy.start()
        third.append(copy)
    for d in range(place.chips):
        came = place.chip_at(-d) * 2 + 1 - place.core
        send(
            full.at[came], full.at[came], ss.at[d], sr.at[d], (place.sibling, time)
        ).wait_recv()
    for copy in first + second + third:
        copy.wait_send()


def pair_sems(*counts):
    return [pltpu.SemaphoreType.DMA((n,)) for n in counts for _ in range(2)]


def pairs(sems):
    return [(sems[2 * k], sems[2 * k + 1]) for k in range(len(sems) // 2)]


def old_kernel(
    tiles, times, offsets_ref, weights_hbm, old_hbm, full_ref, sorted_ref,
    weights, old, chunks, local, *sems
):
    place = Place(tiles, times)
    fetch_old = pltpu.make_async_copy(old_hbm, old, local.at[0])
    fetch_old.start()
    fetch_weights = pltpu.make_async_copy(weights_hbm, weights, local.at[1])
    fetch_weights.start()
    place.signal()
    fetch_old.wait()
    for i in range(times // 2):
        part = old[:, i * LANES : (i + 1) * LANES].astype(jnp.float32)
        even, odd = chunks_of(part[:PACK], part[PACK:])
        chunks[2 * i] = even.astype(jnp.bfloat16)
        chunks[2 * i + 1] = odd.astype(jnp.bfloat16)
    place.wait()

    def meanwhile():
        fetch_weights.wait()
        sort_weights(offsets_ref, weights, sorted_ref)

    spread(place, chunks, full_ref, pairs(sems), meanwhile)


def remote_params(identity, limit):
    return pltpu.CompilerParams(
        vmem_limit_bytes=limit * 2**20, collective_id=identity, has_side_effects=True
    )


def spread_old(traces_old, offsets, weights):
    tiles, times = lax.axis_size("tile"), lax.axis_size("tm")
    count, rows, cols = weights.shape
    return pl.pallas_call(
        functools.partial(old_kernel, tiles, times),
        out_shape=[
            jax.ShapeDtypeStruct((tiles, times * PACK, LANES), jnp.bfloat16),
            jax.ShapeDtypeStruct((count * PLANES, rows, LANES), jnp.float32),
        ],
        in_specs=[whole(SMEM), whole(pltpu.MemorySpace.HBM), whole(pltpu.MemorySpace.HBM)],
        out_specs=[whole()] * 2,
        scratch_shapes=[
            pltpu.VMEM(weights.shape, weights.dtype),
            pltpu.VMEM(traces_old.shape, traces_old.dtype),
            pltpu.VMEM((times, PACK, LANES), jnp.bfloat16),
            pltpu.SemaphoreType.DMA((2,)),
        ]
        + pair_sems(times, tiles // 2, tiles // 2),
        compiler_params=remote_params(0, 54),
        cost_estimate=cost(15),
        name="spread_old",
    )(offsets, weights, traces_old)


def exchange_kernel(
    tiles, times, taps_ref, old_ref, sums_ref, full_ref, fresh_ref,
    pair_buf, x_send, x_buf, owner_send, owner_buf, stacked, spare, band, chunks, *sems
):
    place = Place(tiles, times)
    (ps, pr), (xs, xr), (ts, tr), *rest = pairs(sems)
    chips, tile, time, core = place.chips, place.tile, place.time, place.core
    rows = times * PACK
    place.signal()
    place.wait()
    to_pair = []
    for d in [*place.chip_steps, 0]:
        at = place.chip_at(d)
        copy = send(
            sums_ref.at[1 - core, at], pair_buf.at[at], ps.at[d], pr.at[d], (place.sibling, time)
        )
        copy.start()
        to_pair.append((d, at, copy))
    to_chip = []
    mine = None
    for d, at, copy in to_pair:
        copy.wait_recv()
        total = sums_ref[core, at].astype(jnp.float32) + pair_buf[at].astype(jnp.float32)
        if d:
            x_send[d] = total.astype(jnp.bfloat16)
            out = send(x_send.at[d], x_buf.at[d], xs.at[d], xr.at[d], (at * 2 + core, time))
            out.start()
            to_chip.append(out)
        else:
            mine = total
    for d, copy in reversed(list(zip(place.chip_steps, to_chip))):
        copy.wait_recv()
        mine += x_buf[d].astype(jnp.float32)
    frames = rows * LANES // (2 * PACK * times)
    each = BLOCK // (2 * PACK)
    for q in range(rows // frames):
        turned = mine[q * frames : (q + 1) * frames].T
        for k in range(each):
            top = turned[2 * k * PACK : (2 * k + 1) * PACK]
            bottom = turned[(2 * k + 1) * PACK : (2 * k + 2) * PACK]
            owner_send[q * each + k] = jnp.concatenate([top, bottom], axis=1)
    to_owner = []
    for d in range(1, times):
        peer = place.time_at(d)
        copy = send(owner_send.at[peer], owner_buf.at[time], ts.at[d], tr.at[d], (tile, peer))
        copy.start()
        to_owner.append(copy)
    owner_buf[time] = owner_send[time]

    spare[...] = jnp.zeros_like(spare)
    spare[0:1, 0 : taps_ref.shape[1]] = taps_ref[...]
    wide = jnp.broadcast_to(spare[0:1, :], (2 * LANES, 2 * LANES))
    band[...] = pltpu.roll(wide, LANES, 1, stride=1, stride_axis=0)[:, :LANES]

    high = mine[rows : rows + PACK]
    both = high + pltpu.roll(high, PACK - PACK // 2, 0)
    block = lax.rem(time * 2 * PACK, BLOCK)
    line = lax.broadcasted_iota(jnp.int32, (PACK, LANES), 0)
    lane = lax.broadcasted_iota(jnp.int32, (PACK, LANES), 1)
    row = jnp.sum(
        jnp.where(line == time // (BLOCK // (2 * PACK)), both, 0.0), axis=0, keepdims=True
    )
    columns = [
        jnp.sum(jnp.where(lane == line + block + k * PACK, row, 0.0), axis=1, keepdims=True)
        for k in range(2)
    ]
    divisor = jnp.where(lane < HALF_LANES, columns[0], columns[1]) + RIDGE

    for d in range(1, times):
        came = place.time_at(d, -1)
        send(
            owner_send.at[came], owner_buf.at[came], ts.at[d], tr.at[d], (tile, came)
        ).wait_recv()
    update = [jnp.zeros((PACK, LANES), jnp.float32)]
    for i in range(times // 2):
        part = old_ref[:, i * LANES : (i + 1) * LANES].astype(jnp.float32)
        for k, old in enumerate(chunks_of(part[:PACK], part[PACK:])):
            update.append(old + owner_buf[2 * i + k] / divisor)
    update.append(jnp.zeros((PACK, LANES), jnp.float32))
    steps = times // 2
    lines = [
        (join_low(update[2 * i], update[2 * i + 1]), join_high(update[2 * i], update[2 * i + 1]))
        for i in range(steps + 1)
    ]
    for i in range(steps):
        for k in range(2):
            at = slice((2 * i + k) * PACK, (2 * i + k + 1) * PACK)
            stacked[at, :LANES] = lines[i][k]
            stacked[at, LANES:] = lines[i + 1][k]
    made = jnp.dot(
        stacked[...],
        band[...],
        precision=lax.Precision.HIGHEST,
        preferred_element_type=jnp.float32,
    )
    made = jnp.maximum(made, 0.0)
    for i in range(steps):
        part = made[2 * i * PACK : (2 * i + 2) * PACK]
        fresh_ref[:, i * LANES : (i + 1) * LANES] = part.astype(jnp.bfloat16)
        even, odd = chunks_of(part[:PACK], part[PACK:])
        chunks[2 * i] = even.astype(jnp.bfloat16)
        chunks[2 * i + 1] = odd.astype(jnp.bfloat16)
    spread(place, chunks, full_ref, rest)
    for copy in [c for _, _, c in to_pair] + to_chip + to_owner:
        copy.wait_send()


def exchange(taps, traces_old, sums):
    tiles, times = lax.axis_size("tile"), lax.axis_size("tm")
    chips = tiles // 2
    rows = times * PACK
    group = (rows + PACK, LANES)
    return pl.pallas_call(
        functools.partial(exchange_kernel, tiles, times),
        out_shape=[
            jax.ShapeDtypeStruct((tiles, rows, LANES), jnp.bfloat16),
            jax.ShapeDtypeStruct(traces_old.shape, jnp.bfloat16),
        ],
        in_specs=[whole()] * 3,
        out_specs=[whole()] * 2,
        scratch_shapes=[
            pltpu.VMEM((chips,) + group, jnp.bfloat16),
            pltpu.VMEM((chips,) + group, jnp.bfloat16),
            pltpu.VMEM((chips,) + group, jnp.bfloat16),
            pltpu.VMEM((times, PACK, LANES), jnp.float32),
            pltpu.VMEM((times, PACK, LANES), jnp.float32),
            pltpu.VMEM((times * PACK, 2 * LANES), jnp.float32),
            pltpu.VMEM((8, 2 * LANES), jnp.float32),
            pltpu.VMEM((2 * LANES, LANES), jnp.float32),
            pltpu.VMEM((times, PACK, LANES), jnp.bfloat16),
        ]
        + pair_sems(chips, chips, times, times, chips, chips),
        compiler_params=remote_params(1, 12),
        cost_estimate=cost(25),
        name="exchange",
    )(taps[None, :], traces_old, sums)


PLANES = 4
REACH = RAD // PLANES
ROLLS = 2 * REACH + 1


def sorting(cols):
    shape = (cols, PLANES * LANES)
    column = lax.broadcasted_iota(jnp.int32, shape, 0)
    place = lax.broadcasted_iota(jnp.int32, shape, 1)
    hit = column == PLANES * lax.rem(place, LANES // 2) + place // LANES
    return hit.astype(jnp.float32).astype(jnp.bfloat16)


def unsorting(cols):
    shape = (PLANES * LANES, 2 * cols)
    place = lax.broadcasted_iota(jnp.int32, shape, 0)
    target = lax.broadcasted_iota(jnp.int32, shape, 1)
    hit = target == lax.rem(place, LANES) // (LANES // 2) * cols + (
        PLANES * lax.rem(place, LANES // 2) + place // LANES
    )
    return hit.astype(jnp.float32).astype(jnp.bfloat16)


def sort_weights(offsets_ref, weights_ref, sorted_ref, each=8):
    count, rows, cols = weights_ref.shape
    sort = sorting(cols)
    column = lax.broadcasted_iota(jnp.int32, (rows, cols), 1)

    def some(step, carry):
        parts = []
        for u in range(each):
            j = step * each + u
            place = column + offsets_ref[1, j]
            parts.append(jnp.where((place >= 0) & (place < cols), weights_ref[j], 0.0))
        left = jnp.concatenate(parts, axis=0)
        total = jnp.zeros((each * rows, PLANES * LANES), jnp.float32)
        for _ in range(3):
            piece = left.astype(jnp.bfloat16)
            total += jnp.dot(piece, sort, preferred_element_type=jnp.float32)
            left = left - piece.astype(jnp.float32)
        for u in range(each):
            for p in range(PLANES):
                sorted_ref[(step * each + u) * PLANES + p] = total[
                    u * rows : (u + 1) * rows, p * LANES : (p + 1) * LANES
                ]
        return carry

    lax.fori_loop(0, count // each, some, 0)


def clean_kernel(
    tiles, offsets_ref, weights_ref, first_ref, third_ref,
    copies_0, copies_1, field, halo, table, sends, recvs
):
    rows, frames, cols = first_ref.shape
    count = offsets_ref.shape[1]
    half = frames // 2
    padded = rows + 2 * RAD
    copies = (copies_0, copies_1)
    tile, time = lax.axis_index("tile"), lax.axis_index("tm")
    below, above = lax.rem(tile + 1, tiles), lax.rem(tile + tiles - 1, tiles)
    barrier = pltpu.get_barrier_semaphore()
    for peer in (below, above):
        pl.semaphore_signal(barrier, inc=1, device_id=(peer, time), device_id_type=MESH)

    sort = sorting(cols)
    lower = lax.broadcasted_iota(jnp.int32, (RAD, half, LANES), 2) < LANES // 2

    def sort_rows(base):
        wide = jnp.dot(
            first_ref[pl.ds(base, RAD)].reshape(RAD * frames, cols),
            sort,
            preferred_element_type=jnp.float32,
        ).reshape(RAD, frames, PLANES * LANES)
        for p in range(PLANES):
            plane = wide[:, :, p * LANES : (p + 1) * LANES]
            field[0, pl.ds(base, RAD), p] = jnp.where(
                lower, plane[:, :half], plane[:, half:]
            ).astype(jnp.bfloat16)

    def halo_copies(turn):
        return [
            send(
                field.at[turn, pl.ds(start, RAD)],
                halo.at[turn, side],
                sends.at[turn, side],
                recvs.at[turn, side],
                (peer, time),
            )
            for side, start, peer in ((0, rows - RAD, below), (1, 0, above))
        ]

    def roll_plane(turn, p, values, row):
        for s in range(ROLLS):
            shift = (REACH - s) % LANES
            copies[turn][(s * PLANES + p) * padded + row] = (
                pltpu.roll(values, shift, 1) if shift else values
            )

    def roll_own():
        def some(step, carry):
            for u in range(2 * RAD):
                row = step * 2 * RAD + u
                for p in range(PLANES):
                    roll_plane(0, p, field[0, row, p].astype(jnp.float32), RAD + row)
            return carry

        lax.fori_loop(0, rows // (2 * RAD), some, 0)

    def roll_halo(turn):
        for side, edge, base in ((0, tile == 0, 0), (1, tile == tiles - 1, RAD + rows)):
            for row in range(RAD):
                for p in range(PLANES):
                    values = halo[turn, side, row, p].astype(jnp.float32)
                    roll_plane(turn, p, jnp.where(edge, 0.0, values), base + row)

    def run_rows(turn, edges):
        def some(step, carry):
            row = step * RAD + RAD
            if edges:
                row = jnp.where(step < RAD // RAD, step * RAD, step * RAD + rows - 2 * RAD)
            for p in range(PLANES):
                total = [jnp.zeros((half, LANES), jnp.float32) for _ in range(RAD)]
                for j in range(count):
                    k = j * PLANES + p
                    source = copies[turn][pl.ds(table[k] + row, RAD)]
                    for r in range(RAD):
                        total[r] += weights_ref[k, pl.ds(row + r, 1), :] * source[r]
                mine = copies[turn][pl.ds((REACH * PLANES + p) * padded + RAD + row, RAD)]
                for r in range(RAD):
                    out = (mine[r] - total[r]).astype(jnp.bfloat16)
                    field[1 - turn, row + r, p] = out
                    if turn == 0:
                        roll_plane(1, p, out.astype(jnp.float32), RAD + row + r)
            return carry

        lax.fori_loop(0, (2 * RAD if edges else rows - 2 * RAD) // RAD, some, 0)

    sort_rows(0)
    sort_rows(rows - RAD)
    pl.semaphore_wait(barrier, 2)
    for turn in range(2):
        moving = halo_copies(turn)
        for copy in moving:
            copy.start()
        if turn == 0:
            for base in range(RAD, rows - RAD, RAD):
                sort_rows(base)
            for j in range(count):
                for p in range(PLANES):
                    q = p + offsets_ref[1, j] + RAD
                    table[j * PLANES + p] = q * padded + RAD + offsets_ref[0, j]
            roll_own()
        run_rows(turn, False)
        for copy in moving:
            copy.wait()
        roll_halo(turn)
        run_rows(turn, True)

    unsort = unsorting(cols)
    for base in range(0, rows, RAD):
        planes = [field[0, base : base + RAD, p].astype(jnp.float32) for p in range(PLANES)]
        flat = jnp.concatenate(planes, axis=2).reshape(RAD * half, PLANES * LANES)
        back = jnp.dot(flat.astype(jnp.bfloat16), unsort, preferred_element_type=jnp.float32)
        back = back.astype(jnp.bfloat16).reshape(RAD, half, 2 * cols)
        for k in range(2):
            third_ref[base : base + RAD, k * half : (k + 1) * half] = back[
                :, :, k * cols : (k + 1) * cols
            ]


def clean(offsets, weights, first):
    rows, frames, cols = first.shape
    row = (PLANES, frames // 2, LANES)
    copies = pltpu.VMEM((ROLLS * PLANES * (rows + 2 * RAD),) + row[1:], jnp.float32)
    return pl.pallas_call(
        functools.partial(clean_kernel, lax.axis_size("tile")),
        out_shape=jax.ShapeDtypeStruct(first.shape, jnp.bfloat16),
        in_specs=[whole(SMEM), whole(), whole()],
        out_specs=whole(),
        scratch_shapes=[
            copies,
            copies,
            pltpu.VMEM((2, rows) + row, jnp.bfloat16),
            pltpu.VMEM((2, 2, RAD) + row, jnp.bfloat16),
            pltpu.SMEM((PLANES * offsets.shape[1],), jnp.int32),
            pltpu.SemaphoreType.DMA((2, 2)),
            pltpu.SemaphoreType.DMA((2, 2)),
        ],
        compiler_params=remote_params(2, 42),
        cost_estimate=cost(25),
        name="clean",
    )(offsets, weights, first)


def body(movie, footprints, support, cycle_offsets, cycle_weights, owner_map, traces_old, taps):
    tiles, slots = support.shape
    chips, times = lax.axis_size("tile") // 2, lax.axis_size("tm")
    foot = footprints.reshape(tiles, slots, TILE * TILE, BLOCK)
    field = movie.transpose(0, 2, 1)
    blocks, offsets = support.T, cycle_offsets.T
    old_full, weights = spread_old(traces_old, offsets, cycle_weights)
    old_full = old_full.reshape(-1, LANES)
    first = add_image(-1.0, blocks, owner_map, [old_full], foot, field, "first_residual")
    third = clean(offsets, weights, first)
    sums = project(blocks, owner_map, foot, third, chips, times)
    new_full, fresh = exchange(taps, traces_old, sums)
    new_full = new_full.reshape(-1, LANES)
    residual, fresh = add_image(
        1.0, blocks, owner_map, [old_full, new_full], foot, third, "final_residual", (fresh,)
    )
    return (residual.transpose(0, 2, 1), fresh)


def solution(mesh):
    return jax.shard_map(
        body,
        mesh=mesh,
        in_specs=(
            P("tile", None, "tm"),
            P("tile", None, None, None, None),
            P("tile", None),
            P(),
            P(None, "tile", None),
            P(),
            P(("tile", "tm"), None),
            P(),
        ),
        out_specs=(P("tile", None, "tm"), P(("tile", "tm"), None)),
        check_vma=False,
    )
```

```python
import functools
import math

import jax
import jax.numpy as jnp
from jax import lax
from jax.experimental import pallas as pl
from jax.experimental.pallas import tpu as pltpu
from jax.sharding import PartitionSpec as P

TILE = 32
BLOCK = 128
NBLK = 32
RAD = 8
RIDGE = 1.0
GROUP = 4
LANES = 128

SMEM = pltpu.MemorySpace.SMEM


def whole(space=pltpu.MemorySpace.VMEM):
    return pl.BlockSpec(memory_space=space)


def params(limit):
    return pltpu.CompilerParams(vmem_limit_bytes=limit * 2**20)


def cost(microseconds):
    return pl.CostEstimate(
        flops=microseconds * 10**9, bytes_accessed=microseconds * 10**6, transcendentals=0
    )


def block_of(support_ref, owner_ref, tile, slot):
    held = support_ref[slot, tile]
    return held >= 0, owner_ref[jnp.maximum(held, 0)]


def image_kernel(sign, both, support_ref, owner_ref, *refs):
    traces_refs, refs = refs[: 1 + both], refs[1 + both :]
    if both:
        foot_ref, field_ref, fresh_ref, out_ref, fresh_out, images = refs
        fresh_out[...] = fresh_ref[...]
    else:
        foot_ref, field_ref, out_ref, images = refs
    tiles, slots = foot_ref.shape[0], foot_ref.shape[1]
    rows, frames, cols = field_ref.shape
    group = LANES // TILE

    def block(tile, slot):
        live, position = block_of(support_ref, owner_ref, tile, slot)
        at = pl.ds(pl.multiple_of(position * (BLOCK // 2), BLOCK // 2), BLOCK // 2)
        if both:
            old, new = [ref[at, :].astype(jnp.float32) for ref in traces_refs]
            part = unpack(old - new)
        else:
            part = unpack(traces_refs[0][at, :])
        return jnp.where(live, part, jnp.zeros_like(part))

    for strip in range(cols // LANES):
        for inner in range(group):
            tile = strip * group + inner
            images[strip, :, inner * TILE : (inner + 1) * TILE, :] = jnp.dot(
                jnp.concatenate([foot_ref[tile, slot] for slot in range(slots)], axis=1),
                jnp.concatenate([block(tile, slot) for slot in range(slots)], axis=0),
                preferred_element_type=jnp.float32,
            ).reshape(rows, TILE, frames)
        lanes = slice(strip * LANES, (strip + 1) * LANES)
        for row in range(0, rows, 2):
            turned = jnp.concatenate([images[strip, row], images[strip, row + 1]], axis=1).T
            for k in range(2):
                part = turned[k * frames : (k + 1) * frames]
                out_ref[row + k, :, lanes] = (
                    field_ref[row + k, :, lanes].astype(jnp.float32) + sign * part
                ).astype(jnp.bfloat16)


def add_image(sign, support, owner_map, traces, foot, field, name, fresh=()):
    rows, frames, cols = field.shape
    made = pl.pallas_call(
        functools.partial(image_kernel, sign, len(traces) - 1),
        out_shape=[jax.ShapeDtypeStruct(x.shape, jnp.bfloat16) for x in (field, *fresh)],
        in_specs=[whole(SMEM), whole(SMEM)]
        + [whole() for _ in range(len(traces) + 2 + len(fresh))],
        out_specs=[whole() for _ in range(1 + len(fresh))],
        scratch_shapes=[pltpu.VMEM((cols // LANES, rows, LANES, frames), jnp.float32)],
        compiler_params=params(20),
        cost_estimate=cost(5),
        name=name,
    )(support, owner_map, *traces, foot, field, *fresh)
    return made if fresh else made[0]


def project_kernel(
    support_ref, owner_ref, foot_ref, field_ref, packed_ref, view, sums_ref, norms_ref
):
    tiles, slots, pixels, _ = foot_ref.shape
    rows, frames, cols = field_ref.shape
    group = LANES // TILE
    sums_ref[...] = jnp.zeros_like(sums_ref)
    norms_ref[...] = jnp.zeros_like(norms_ref)
    lane = lax.broadcasted_iota(jnp.int32, (frames, LANES), 1)

    def add(tile, slot):
        both = jnp.dot(
            view[tile],
            jnp.concatenate([foot_ref[tile, slot], foot_ref[tile, slot + 1]], axis=1),
            preferred_element_type=jnp.float32,
        )
        for k in range(2):
            live, position = block_of(support_ref, owner_ref, tile, slot + k)
            part = both[:, k * BLOCK : (k + 1) * BLOCK]
            sums_ref[position] += jnp.where(live, part, 0.0)
            wide = foot_ref[tile, slot + k].astype(jnp.float32)
            square = jnp.sum((wide * wide).reshape(pixels // 8, 8, BLOCK), axis=0)
            norms_ref[position] += jnp.where(live, square, 0.0)

    for strip in range(cols // LANES):
        lanes = slice(strip * LANES, (strip + 1) * LANES)

        for step in range(rows // group):
            source = [
                field_ref[step * group + k, :, lanes].astype(jnp.float32) for k in range(group)
            ]
            at = slice(step * LANES, (step + 1) * LANES)
            for t in range(group):
                line = None
                for k in range(group):
                    shift = (k - t) * TILE % LANES
                    moved = pltpu.roll(source[k], shift, 1) if shift else source[k]
                    line = moved if k == 0 else jnp.where(lane >= k * TILE, moved, line)
                view[strip * group + t, :, at] = line.astype(jnp.bfloat16)

        for inner in range(group):
            add(strip * group + inner, 0)

    for tile in range(tiles):
        for slot in range(2, slots, 2):

            @pl.when(support_ref[slot, tile] >= 0)
            def _(tile=tile, slot=slot):
                add(tile, slot)

    each = packed_ref.shape[2] - PACK
    per = each // frames
    for core in range(packed_ref.shape[0]):
        for chip in range(packed_ref.shape[1]):
            base = (2 * chip + core) * per
            packed_ref[core, chip, :each] = (
                sums_ref[base : base + per].reshape(each, BLOCK).astype(jnp.bfloat16)
            )
            lines = [jnp.sum(norms_ref[base + q], axis=0, keepdims=True) for q in range(per)]
            fill = [jnp.zeros((PACK // 2 - per, BLOCK), jnp.float32)]
            norms = jnp.concatenate(lines + fill, axis=0)
            high = norms.astype(jnp.bfloat16).astype(jnp.float32)
            packed_ref[core, chip, each : each + PACK] = jnp.concatenate(
                [high, norms - high], axis=0
            ).astype(jnp.bfloat16)


def project(support, owner_map, foot, field, chips, times):
    rows, frames, cols = field.shape
    return pl.pallas_call(
        project_kernel,
        out_shape=jax.ShapeDtypeStruct((2, chips, times * PACK + PACK, LANES), jnp.bfloat16),
        in_specs=[whole(SMEM), whole(SMEM), whole(), whole()],
        out_specs=whole(),
        scratch_shapes=[
            pltpu.VMEM((foot.shape[0], frames, TILE * TILE), jnp.bfloat16),
            pltpu.VMEM((NBLK, frames, BLOCK), jnp.float32),
            pltpu.VMEM((NBLK, 8, BLOCK), jnp.float32),
        ],
        compiler_params=params(20),
        cost_estimate=cost(7),
        name="project",
    )(support, owner_map, foot, field)


MESH = pl.DeviceIdType.MESH
PACK = 16
HALF_LANES = LANES // 2


def low_lanes():
    return lax.broadcasted_iota(jnp.int32, (PACK, LANES), 1) < HALF_LANES


def join_low(left, right):
    return jnp.where(low_lanes(), left, pltpu.roll(right, HALF_LANES, 1))


def join_high(left, right):
    return jnp.where(low_lanes(), pltpu.roll(left, HALF_LANES, 1), right)


def chunks_of(top, bottom):
    return join_low(top, bottom), join_high(top, bottom)


def unpack(packed):
    wide = packed.astype(jnp.float32)
    turned = pltpu.roll(wide, HALF_LANES, 1)
    parts = []
    for k in range(packed.shape[0] // PACK):
        rows = slice(k * PACK, (k + 1) * PACK)
        parts += [wide[rows, :HALF_LANES], turned[rows, :HALF_LANES]]
    return jnp.concatenate(parts, axis=0).astype(jnp.bfloat16)


def far_first(peers, square):
    side = math.isqrt(peers) if square else peers
    if square and side * side != peers:
        side = peers
    steps = [(a, b) for a in range(peers // side) for b in range(side)][1:]

    def hops(step):
        return min(step[0], peers // side - step[0]) + min(step[1], side - step[1])

    return side, sorted(steps, key=hops, reverse=True)


class Place:
    def __init__(self, tiles, times):
        self.chips, self.times = tiles // 2, times
        self.tile, self.time = lax.axis_index("tile"), lax.axis_index("tm")
        self.chip, self.core = self.tile // 2, lax.rem(self.tile, 2)
        self.sibling = self.chip * 2 + 1 - self.core
        self.side, self.time_steps = far_first(times, True)
        self.chip_steps = [b for _, b in far_first(self.chips, False)[1]]

    def chip_at(self, step):
        return lax.rem(self.chip + step + self.chips, self.chips)

    def time_at(self, d, sign=1):
        a, b = self.time_steps[d - 1]
        rings = self.times // self.side
        return lax.rem(self.time // self.side + sign * a + rings, rings) * self.side + lax.rem(
            lax.rem(self.time, self.side) + sign * b + self.side, self.side
        )

    def signal(self):
        barrier = pltpu.get_barrier_semaphore()
        peers = [(self.tile, self.time_at(d)) for d in range(1, self.times)]
        peers += [(self.chip_at(d) * 2 + self.core, self.time) for d in self.chip_steps]
        peers += [(self.sibling, self.time)]
        for peer in peers:
            pl.semaphore_signal(barrier, inc=1, device_id=peer, device_id_type=MESH)
        self.peers = len(peers)

    def wait(self):
        pl.semaphore_wait(pltpu.get_barrier_semaphore(), self.peers)


def send(source, target, send_sem, recv_sem, device):
    return pltpu.make_async_remote_copy(
        src_ref=source,
        dst_ref=target,
        send_sem=send_sem,
        recv_sem=recv_sem,
        device_id=device,
        device_id_type=MESH,
    )


def spread(place, chunks, full, sems, meanwhile=None):
    (ts, tr), (xs, xr), (ss, sr) = sems
    tile, time = place.tile, place.time

    def rows(index):
        return pl.ds(pl.multiple_of(index * PACK, PACK), PACK)

    first = []
    for d in range(1, place.times):
        peer = place.time_at(d)
        copy = send(
            chunks.at[peer], full.at[tile, rows(time)], ts.at[d], tr.at[d], (tile, peer)
        )
        copy.start()
        first.append(copy)
    full[tile, rows(time)] = chunks[time]
    if meanwhile:
        meanwhile()
    for d, copy in enumerate(first, 1):
        came = place.time_at(d, -1)
        send(
            chunks.at[time], full.at[tile, rows(came)], ts.at[d], tr.at[d], (tile, came)
        ).wait_recv()
    second = []
    for d in place.chip_steps:
        copy = send(
            full.at[tile],
            full.at[tile],
            xs.at[d],
            xr.at[d],
            (place.chip_at(d) * 2 + place.core, time),
        )
        copy.start()
        second.append(copy)
    third = []
    for d in [0, *reversed(place.chip_steps)]:
        came = place.chip_at(-d) * 2 + place.core
        if d:
            send(full.at[came], full.at[came], xs.at[d], xr.at[d], (came, time)).wait_recv()
        copy = send(
            full.at[came], full.at[came], ss.at[d], sr.at[d], (place.sibling, time)
        )
        copy.start()
        third.append(copy)
    for d in range(place.chips):
        came = place.chip_at(-d) * 2 + 1 - place.core
        send(
            full.at[came], full.at[came], ss.at[d], sr.at[d], (place.sibling, time)
        ).wait_recv()
    for copy in first + second + third:
        copy.wait_send()


def pair_sems(*counts):
    return [pltpu.SemaphoreType.DMA((n,)) for n in counts for _ in range(2)]


def pairs(sems):
    return [(sems[2 * k], sems[2 * k + 1]) for k in range(len(sems) // 2)]


def old_kernel(
    tiles, times, offsets_ref, weights_hbm, old_hbm, full_ref, sorted_ref,
    weights, old, chunks, local, *sems
):
    place = Place(tiles, times)
    fetch_old = pltpu.make_async_copy(old_hbm, old, local.at[0])
    fetch_old.start()
    fetch_weights = pltpu.make_async_copy(weights_hbm, weights, local.at[1])
    fetch_weights.start()
    place.signal()
    fetch_old.wait()
    for i in range(times // 2):
        part = old[:, i * LANES : (i + 1) * LANES].astype(jnp.float32)
        even, odd = chunks_of(part[:PACK], part[PACK:])
        chunks[2 * i] = even.astype(jnp.bfloat16)
        chunks[2 * i + 1] = odd.astype(jnp.bfloat16)
    place.wait()

    def meanwhile():
        fetch_weights.wait()
        sort_weights(offsets_ref, weights, sorted_ref)

    spread(place, chunks, full_ref, pairs(sems), meanwhile)


def remote_params(identity, limit):
    return pltpu.CompilerParams(
        vmem_limit_bytes=limit * 2**20, collective_id=identity, has_side_effects=True
    )


def spread_old(traces_old, offsets, weights):
    tiles, times = lax.axis_size("tile"), lax.axis_size("tm")
    count, rows, cols = weights.shape
    return pl.pallas_call(
        functools.partial(old_kernel, tiles, times),
        out_shape=[
            jax.ShapeDtypeStruct((tiles, times * PACK, LANES), jnp.bfloat16),
            jax.ShapeDtypeStruct((count * PLANES, rows, LANES), jnp.float32),
        ],
        in_specs=[whole(SMEM), whole(pltpu.MemorySpace.HBM), whole(pltpu.MemorySpace.HBM)],
        out_specs=[whole()] * 2,
        scratch_shapes=[
            pltpu.VMEM(weights.shape, weights.dtype),
            pltpu.VMEM(traces_old.shape, traces_old.dtype),
            pltpu.VMEM((times, PACK, LANES), jnp.bfloat16),
            pltpu.SemaphoreType.DMA((2,)),
        ]
        + pair_sems(times, tiles // 2, tiles // 2),
        compiler_params=remote_params(0, 54),
        cost_estimate=cost(15),
        name="spread_old",
    )(offsets, weights, traces_old)


def exchange_kernel(
    tiles, times, taps_ref, old_ref, sums_ref, full_ref, fresh_ref,
    pair_buf, x_send, x_buf, owner_send, owner_buf, stacked, spare, band, chunks, *sems
):
    place = Place(tiles, times)
    (ps, pr), (xs, xr), (ts, tr), *rest = pairs(sems)
    chips, tile, time, core = place.chips, place.tile, place.time, place.core
    rows = times * PACK
    place.signal()
    place.wait()
    to_pair = []
    for d in [*place.chip_steps, 0]:
        at = place.chip_at(d)
        copy = send(
            sums_ref.at[1 - core, at], pair_buf.at[at], ps.at[d], pr.at[d], (place.sibling, time)
        )
        copy.start()
        to_pair.append((d, at, copy))
    to_chip = []
    mine = None
    for d, at, copy in to_pair:
        copy.wait_recv()
        total = sums_ref[core, at].astype(jnp.float32) + pair_buf[at].astype(jnp.float32)
        if d:
            x_send[d] = total.astype(jnp.bfloat16)
            out = send(x_send.at[d], x_buf.at[d], xs.at[d], xr.at[d], (at * 2 + core, time))
            out.start()
            to_chip.append(out)
        else:
            mine = total
    for d, copy in reversed(list(zip(place.chip_steps, to_chip))):
        copy.wait_recv()
        mine += x_buf[d].astype(jnp.float32)
    frames = rows * LANES // (2 * PACK * times)
    each = BLOCK // (2 * PACK)
    for q in range(rows // frames):
        turned = mine[q * frames : (q + 1) * frames].T
        for k in range(each):
            top = turned[2 * k * PACK : (2 * k + 1) * PACK]
            bottom = turned[(2 * k + 1) * PACK : (2 * k + 2) * PACK]
            both = jnp.concatenate([top, bottom], axis=1)
            owner_send[q * each + k] = both.astype(jnp.bfloat16)
    to_owner = []
    for d in range(1, times):
        peer = place.time_at(d)
        copy = send(owner_send.at[peer], owner_buf.at[time], ts.at[d], tr.at[d], (tile, peer))
        copy.start()
        to_owner.append(copy)
    owner_buf[time] = owner_send[time]

    spare[...] = jnp.zeros_like(spare)
    spare[0:1, 0 : taps_ref.shape[1]] = taps_ref[...]
    wide = jnp.broadcast_to(spare[0:1, :], (2 * LANES, 2 * LANES))
    band[...] = pltpu.roll(wide, LANES, 1, stride=1, stride_axis=0)[:, :LANES]

    high = mine[rows : rows + PACK]
    both = high + pltpu.roll(high, PACK - PACK // 2, 0)
    block = lax.rem(time * 2 * PACK, BLOCK)
    line = lax.broadcasted_iota(jnp.int32, (PACK, LANES), 0)
    lane = lax.broadcasted_iota(jnp.int32, (PACK, LANES), 1)
    row = jnp.sum(
        jnp.where(line == time // (BLOCK // (2 * PACK)), both, 0.0), axis=0, keepdims=True
    )
    columns = [
        jnp.sum(jnp.where(lane == line + block + k * PACK, row, 0.0), axis=1, keepdims=True)
        for k in range(2)
    ]
    divisor = jnp.where(lane < HALF_LANES, columns[0], columns[1]) + RIDGE

    for d in range(1, times):
        came = place.time_at(d, -1)
        send(
            owner_send.at[came], owner_buf.at[came], ts.at[d], tr.at[d], (tile, came)
        ).wait_recv()
    update = [jnp.zeros((PACK, LANES), jnp.float32)]
    for i in range(times // 2):
        part = old_ref[:, i * LANES : (i + 1) * LANES].astype(jnp.float32)
        for k, old in enumerate(chunks_of(part[:PACK], part[PACK:])):
            update.append(old + owner_buf[2 * i + k].astype(jnp.float32) / divisor)
    update.append(jnp.zeros((PACK, LANES), jnp.float32))
    steps = times // 2
    lines = [
        (join_low(update[2 * i], update[2 * i + 1]), join_high(update[2 * i], update[2 * i + 1]))
        for i in range(steps + 1)
    ]
    for i in range(steps):
        for k in range(2):
            at = slice((2 * i + k) * PACK, (2 * i + k + 1) * PACK)
            stacked[at, :LANES] = lines[i][k]
            stacked[at, LANES:] = lines[i + 1][k]
    made = jnp.dot(
        stacked[...],
        band[...],
        precision=lax.Precision.HIGHEST,
        preferred_element_type=jnp.float32,
    )
    made = jnp.maximum(made, 0.0)
    for i in range(steps):
        part = made[2 * i * PACK : (2 * i + 2) * PACK]
        fresh_ref[:, i * LANES : (i + 1) * LANES] = part.astype(jnp.bfloat16)
        even, odd = chunks_of(part[:PACK], part[PACK:])
        chunks[2 * i] = even.astype(jnp.bfloat16)
        chunks[2 * i + 1] = odd.astype(jnp.bfloat16)
    spread(place, chunks, full_ref, rest)
    for copy in [c for _, _, c in to_pair] + to_chip + to_owner:
        copy.wait_send()


def exchange(taps, traces_old, sums):
    tiles, times = lax.axis_size("tile"), lax.axis_size("tm")
    chips = tiles // 2
    rows = times * PACK
    group = (rows + PACK, LANES)
    return pl.pallas_call(
        functools.partial(exchange_kernel, tiles, times),
        out_shape=[
            jax.ShapeDtypeStruct((tiles, rows, LANES), jnp.bfloat16),
            jax.ShapeDtypeStruct(traces_old.shape, jnp.bfloat16),
        ],
        in_specs=[whole()] * 3,
        out_specs=[whole()] * 2,
        scratch_shapes=[
            pltpu.VMEM((chips,) + group, jnp.bfloat16),
            pltpu.VMEM((chips,) + group, jnp.bfloat16),
            pltpu.VMEM((chips,) + group, jnp.bfloat16),
            pltpu.VMEM((times, PACK, LANES), jnp.bfloat16),
            pltpu.VMEM((times, PACK, LANES), jnp.bfloat16),
            pltpu.VMEM((times * PACK, 2 * LANES), jnp.float32),
            pltpu.VMEM((8, 2 * LANES), jnp.float32),
            pltpu.VMEM((2 * LANES, LANES), jnp.float32),
            pltpu.VMEM((times, PACK, LANES), jnp.bfloat16),
        ]
        + pair_sems(chips, chips, times, times, chips, chips),
        compiler_params=remote_params(1, 12),
        cost_estimate=cost(25),
        name="exchange",
    )(taps[None, :], traces_old, sums)


PLANES = 4
REACH = RAD // PLANES
ROLLS = 2 * REACH + 1


def sorting(cols):
    shape = (cols, PLANES * LANES)
    column = lax.broadcasted_iota(jnp.int32, shape, 0)
    place = lax.broadcasted_iota(jnp.int32, shape, 1)
    hit = column == PLANES * lax.rem(place, LANES // 2) + place // LANES
    return hit.astype(jnp.float32).astype(jnp.bfloat16)


def unsorting(cols):
    shape = (PLANES * LANES, 2 * cols)
    place = lax.broadcasted_iota(jnp.int32, shape, 0)
    target = lax.broadcasted_iota(jnp.int32, shape, 1)
    hit = target == lax.rem(place, LANES) // (LANES // 2) * cols + (
        PLANES * lax.rem(place, LANES // 2) + place // LANES
    )
    return hit.astype(jnp.float32).astype(jnp.bfloat16)


def sort_weights(offsets_ref, weights_ref, sorted_ref, each=8):
    count, rows, cols = weights_ref.shape
    sort = sorting(cols)
    column = lax.broadcasted_iota(jnp.int32, (rows, cols), 1)

    def some(step, carry):
        parts = []
        for u in range(each):
            j = step * each + u
            place = column + offsets_ref[1, j]
            parts.append(jnp.where((place >= 0) & (place < cols), weights_ref[j], 0.0))
        left = jnp.concatenate(parts, axis=0)
        total = jnp.zeros((each * rows, PLANES * LANES), jnp.float32)
        for _ in range(3):
            piece = left.astype(jnp.bfloat16)
            total += jnp.dot(piece, sort, preferred_element_type=jnp.float32)
            left = left - piece.astype(jnp.float32)
        for u in range(each):
            for p in range(PLANES):
                sorted_ref[(step * each + u) * PLANES + p] = total[
                    u * rows : (u + 1) * rows, p * LANES : (p + 1) * LANES
                ]
        return carry

    lax.fori_loop(0, count // each, some, 0)


def clean_kernel(
    tiles, offsets_ref, weights_ref, first_ref, third_ref,
    copies_0, copies_1, field, halo, table, sends, recvs
):
    rows, frames, cols = first_ref.shape
    count = offsets_ref.shape[1]
    half = frames // 2
    padded = rows + 2 * RAD
    copies = (copies_0, copies_1)
    tile, time = lax.axis_index("tile"), lax.axis_index("tm")
    below, above = lax.rem(tile + 1, tiles), lax.rem(tile + tiles - 1, tiles)
    barrier = pltpu.get_barrier_semaphore()
    for peer in (below, above):
        pl.semaphore_signal(barrier, inc=1, device_id=(peer, time), device_id_type=MESH)

    sort = sorting(cols)
    lower = lax.broadcasted_iota(jnp.int32, (RAD, half, LANES), 2) < LANES // 2

    def sort_rows(base):
        wide = jnp.dot(
            first_ref[pl.ds(base, RAD)].reshape(RAD * frames, cols),
            sort,
            preferred_element_type=jnp.float32,
        ).reshape(RAD, frames, PLANES * LANES)
        for p in range(PLANES):
            plane = wide[:, :, p * LANES : (p + 1) * LANES]
            field[0, pl.ds(base, RAD), p] = jnp.where(
                lower, plane[:, :half], plane[:, half:]
            ).astype(jnp.bfloat16)

    def halo_copies(turn):
        return [
            send(
                field.at[turn, pl.ds(start, RAD)],
                halo.at[turn, side],
                sends.at[turn, side],
                recvs.at[turn, side],
                (peer, time),
            )
            for side, start, peer in ((0, rows - RAD, below), (1, 0, above))
        ]

    def roll_plane(turn, p, values, row):
        for s in range(ROLLS):
            shift = (REACH - s) % LANES
            copies[turn][(s * PLANES + p) * padded + row] = (
                pltpu.roll(values, shift, 1) if shift else values
            )

    def roll_own():
        def some(step, carry):
            for u in range(2 * RAD):
                row = step * 2 * RAD + u
                for p in range(PLANES):
                    roll_plane(0, p, field[0, row, p].astype(jnp.float32), RAD + row)
            return carry

        lax.fori_loop(0, rows // (2 * RAD), some, 0)

    def roll_halo(turn):
        for side, edge, base in ((0, tile == 0, 0), (1, tile == tiles - 1, RAD + rows)):
            for row in range(RAD):
                for p in range(PLANES):
                    values = halo[turn, side, row, p].astype(jnp.float32)
                    roll_plane(turn, p, jnp.where(edge, 0.0, values), base + row)

    def run_rows(turn, edges):
        def some(step, carry):
            row = step * RAD + RAD
            if edges:
                row = jnp.where(step < RAD // RAD, step * RAD, step * RAD + rows - 2 * RAD)
            for p in range(PLANES):
                total = [jnp.zeros((half, LANES), jnp.float32) for _ in range(RAD)]
                for j in range(count):
                    k = j * PLANES + p
                    source = copies[turn][pl.ds(table[k] + row, RAD)]
                    for r in range(RAD):
                        total[r] += weights_ref[k, pl.ds(row + r, 1), :] * source[r]
                mine = copies[turn][pl.ds((REACH * PLANES + p) * padded + RAD + row, RAD)]
                for r in range(RAD):
                    out = (mine[r] - total[r]).astype(jnp.bfloat16)
                    field[1 - turn, row + r, p] = out
                    if turn == 0:
                        roll_plane(1, p, out.astype(jnp.float32), RAD + row + r)
            return carry

        lax.fori_loop(0, (2 * RAD if edges else rows - 2 * RAD) // RAD, some, 0)

    sort_rows(0)
    sort_rows(rows - RAD)
    pl.semaphore_wait(barrier, 2)
    for turn in range(2):
        moving = halo_copies(turn)
        for copy in moving:
            copy.start()
        if turn == 0:
            for base in range(RAD, rows - RAD, RAD):
                sort_rows(base)
            for j in range(count):
                for p in range(PLANES):
                    q = p + offsets_ref[1, j] + RAD
                    table[j * PLANES + p] = q * padded + RAD + offsets_ref[0, j]
            roll_own()
        run_rows(turn, False)
        for copy in moving:
            copy.wait()
        roll_halo(turn)
        run_rows(turn, True)

    unsort = unsorting(cols)
    for base in range(0, rows, RAD):
        planes = [field[0, base : base + RAD, p].astype(jnp.float32) for p in range(PLANES)]
        flat = jnp.concatenate(planes, axis=2).reshape(RAD * half, PLANES * LANES)
        back = jnp.dot(flat.astype(jnp.bfloat16), unsort, preferred_element_type=jnp.float32)
        back = back.astype(jnp.bfloat16).reshape(RAD, half, 2 * cols)
        for k in range(2):
            third_ref[base : base + RAD, k * half : (k + 1) * half] = back[
                :, :, k * cols : (k + 1) * cols
            ]


def clean(offsets, weights, first):
    rows, frames, cols = first.shape
    row = (PLANES, frames // 2, LANES)
    copies = pltpu.VMEM((ROLLS * PLANES * (rows + 2 * RAD),) + row[1:], jnp.float32)
    return pl.pallas_call(
        functools.partial(clean_kernel, lax.axis_size("tile")),
        out_shape=jax.ShapeDtypeStruct(first.shape, jnp.bfloat16),
        in_specs=[whole(SMEM), whole(), whole()],
        out_specs=whole(),
        scratch_shapes=[
            copies,
            copies,
            pltpu.VMEM((2, rows) + row, jnp.bfloat16),
            pltpu.VMEM((2, 2, RAD) + row, jnp.bfloat16),
            pltpu.SMEM((PLANES * offsets.shape[1],), jnp.int32),
            pltpu.SemaphoreType.DMA((2, 2)),
            pltpu.SemaphoreType.DMA((2, 2)),
        ],
        compiler_params=remote_params(2, 42),
        cost_estimate=cost(25),
        name="clean",
    )(offsets, weights, first)


def body(movie, footprints, support, cycle_offsets, cycle_weights, owner_map, traces_old, taps):
    tiles, slots = support.shape
    chips, times = lax.axis_size("tile") // 2, lax.axis_size("tm")
    foot = footprints.reshape(tiles, slots, TILE * TILE, BLOCK)
    field = movie.transpose(0, 2, 1)
    blocks, offsets = support.T, cycle_offsets.T
    old_full, weights = spread_old(traces_old, offsets, cycle_weights)
    old_full = old_full.reshape(-1, LANES)
    first = add_image(-1.0, blocks, owner_map, [old_full], foot, field, "first_residual")
    third = clean(offsets, weights, first)
    sums = project(blocks, owner_map, foot, third, chips, times)
    new_full, fresh = exchange(taps, traces_old, sums)
    new_full = new_full.reshape(-1, LANES)
    residual, fresh = add_image(
        1.0, blocks, owner_map, [old_full, new_full], foot, third, "final_residual", (fresh,)
    )
    return (residual.transpose(0, 2, 1), fresh)


def solution(mesh):
    return jax.shard_map(
        body,
        mesh=mesh,
        in_specs=(
            P("tile", None, "tm"),
            P("tile", None, None, None, None),
            P("tile", None),
            P(),
            P(None, "tile", None),
            P(),
            P(("tile", "tm"), None),
            P(),
        ),
        out_specs=(P("tile", None, "tm"), P(("tile", "tm"), None)),
        check_vma=False,
    )
```
